32 devices in a mesh: dp: 4 (over x, core), tp: 8 (over z, y).
Axes of the slice: x: 2, y: 2, z: 4, core: 2. Of those that a mesh axis runs over, the one named last changes fastest.
Arguments:
- qkv_master: float32 [5120, 7168], P(('dp', 'tp')), may hold values from -0.078125 to 0.078125
- qkv_first: float32 [5120, 7168], P(('dp', 'tp')), may hold values from -0.75 to 0.75
- qkv_second: float32 [5120, 7168], P(('dp', 'tp')), may hold values from 0.001 to 0.1
- qkv_grad: bfloat16 [5120, 7168], P(('dp', 'tp')), may hold values from -6 to 6
- out_master: float32 [5120, 5120], P(('dp', 'tp')), may hold values from -0.078125 to 0.078125
- out_first: float32 [5120, 5120], P(('dp', 'tp')), may hold values from -0.75 to 0.75
- out_second: float32 [5120, 5120], P(('dp', 'tp')), may hold values from 0.001 to 0.1
- out_grad: bfloat16 [5120, 5120], P(('dp', 'tp')), may hold values from -6 to 6
- norm_gain: float32 [5120], replicated, may hold values from 0.1 to 1.9
- embed_table: bfloat16 [76032, 5120], P(('dp', 'tp')), may hold values from -6 to 6
- cache_keys: bfloat16 [32, 2048, 1024], P('dp', 'tp'), may hold values from -720 to 720
- cache_values: bfloat16 [32, 2048, 1024], P('dp', 'tp'), may hold values from -6 to 6
- cache_lengths: int32 [32], P('dp'), may hold values from 1 to 2048, as said below
- token_ids: int32 [32, 2], replicated, may hold values from 0 to 76031
Outputs:
- qkv_master_new: float32 [5120, 7168], P(('dp', 'tp'))
- qkv_first_new: float32 [5120, 7168], P(('dp', 'tp'))
- qkv_second_new: float32 [5120, 7168], P(('dp', 'tp'))
- out_master_new: float32 [5120, 5120], P(('dp', 'tp'))
- out_first_new: float32 [5120, 5120], P(('dp', 'tp'))
- out_second_new: float32 [5120, 5120], P(('dp', 'tp'))
- layer_out: bfloat16 [32, 2, 5120], P('dp', None, 'tp')
The draws below stay inside these ranges and needn't reach their ends.
Inputs may be any that keep to these rules, and one draw needn't show every extreme that they name: `cache_lengths`: row 0 has all 2048 positions live and row 1 only one.
All inputs are finite; a program needn't handle non-finite values.
Results may differ from the reference program's by a relative error of at most 0.0035.
The reference program's roundings to bfloat16 on the way (of `inputs`, `normed`, `projected` and `attended`) count: a program that leaves them out, or rounds other values in their place, can miss the bound.
Values may be sent and summed in bfloat16 or wider, within the bound.
No kernel may reach another device: no remote copies, remote signals or barrier semaphores. Data moves between devices by JAX's collectives and lax.ppermute only.
A program may use at most 256 MiB of HBM per device.

```python
import math
import jax
import jax.numpy as jnp
from jax import lax

D = 5120
HEADS = 40
KV_HEADS = 8
HEAD = 128
VOCAB = 76032
CACHE = 2048
QKV = 7168
ROWS = 32


def draw_cache_keys(key, part):
    key = jax.random.fold_in(key, 11)
    key_base = jax.random.fold_in(key, 0)
    key_scale = jax.random.fold_in(key, 3)
    shape = (ROWS, CACHE, KV_HEADS * HEAD)
    row_index = jnp.arange(ROWS, dtype=jnp.int32)
    scaled = row_index % 4 >= 2
    level = jnp.exp(jax.random.uniform(key_scale, (ROWS,), jnp.float32, jnp.log(30.0), jnp.log(120.0)))
    row_factor = jnp.where(scaled, level, 1.0)[:, None, None]
    base = jnp.clip(jax.random.normal(key_base, shape, jnp.float32), -6.0, 6.0)
    return (base * row_factor).astype(jnp.bfloat16)


def draw_cache_lengths(key, part):
    key = jax.random.fold_in(key, 5)
    drawn = jax.random.randint(key, (ROWS,), 1, CACHE + 1, dtype=jnp.int32)
    position = jnp.arange(ROWS, dtype=jnp.int32)
    drawn = jnp.where(position == 0, CACHE, drawn)
    return jnp.where(position == 1, 1, drawn).astype(jnp.int32)


def place_ends(values, own_key, smallest, high):
    spot = [jax.random.randint(jax.random.fold_in(own_key, axis), (), 0, length) for axis, length in enumerate(values.shape)]
    widest = values.shape.index(max(values.shape))
    neighbour = spot[:widest] + [(spot[widest] + 1) % values.shape[widest]] + spot[widest + 1:]
    return values.at[tuple(spot)].set(smallest).at[tuple(neighbour)].set(high)


def level_of(own_key, dims, cuts, low, top_value):
    level, own = 1.0, jax.random.fold_in(own_key, 6)
    for axis_at, shards_of in cuts:
        steps = jnp.exp(jax.random.uniform(jax.random.fold_in(own, axis_at), (shards_of,), jnp.float32, low / len(cuts), top_value / len(cuts)))
        level = level * jnp.repeat(steps, dims[axis_at] // shards_of).reshape([-1 if axis == axis_at else 1 for axis in range(len(dims))])
    return level


def noise(rng, dims, width, bound, shards=(), kind=jnp.bfloat16):
    result = width * jax.random.normal(rng, dims, jnp.float32)
    if shards:
        result = result * level_of(rng, dims, shards, -0.22, 0.18)
    return jnp.clip(result, -bound, bound).astype(kind)


def setup_inputs(seed: int = 0) -> dict:
    arg_keys = jax.random.split(jax.random.key(seed), 15)
    qkv_master = noise(arg_keys[0], (D, QKV), D ** -0.5, 0.078125, ((0, 32),), jnp.float32)
    qkv_first = noise(arg_keys[1], (D, QKV), 0.05, 0.75, ((0, 32),), jnp.float32)
    qkv_second = jnp.clip(jnp.exp(math.log(0.1) - 4.6051702 * jax.random.uniform(arg_keys[2], (D, QKV), jnp.float32) ** level_of(arg_keys[2], (D, QKV), ((0, 32),), -0.2, 0.2)), 0.001, 0.1)
    qkv_grad = noise(arg_keys[3], (D, QKV), 1.0, 6.0, ((0, 32),))
    out_master = noise(arg_keys[4], (D, D), D ** -0.5, 0.078125, ((0, 32),), jnp.float32)
    out_first = noise(arg_keys[5], (D, D), 0.05, 0.75, ((0, 32),), jnp.float32)
    out_second = jnp.clip(jnp.exp(math.log(0.1) - 4.6051702 * jax.random.uniform(arg_keys[6], (D, D), jnp.float32) ** level_of(arg_keys[6], (D, D), ((0, 32),), -0.2, 0.2)), 0.001, 0.1)
    out_grad = noise(arg_keys[7], (D, D), 1.0, 6.0, ((0, 32),))
    norm_gain = jnp.clip(1.0 + 0.18 * jax.random.normal(arg_keys[8], (D,), jnp.float32), 0.1, 1.9)
    embed_table = noise(arg_keys[9], (VOCAB, D), 1.0, 6.0, ((0, 32),))
    cache_keys = draw_cache_keys(jax.random.fold_in(arg_keys[14], 71), 0)
    cache_values = noise(arg_keys[11], (ROWS, CACHE, KV_HEADS * HEAD), 1.0, 6.0, ((0, 4), (1, 8)))
    cache_lengths = draw_cache_lengths(jax.random.fold_in(arg_keys[14], 71), 0)
    token_ids = place_ends(jax.random.randint(arg_keys[13], (ROWS, 2), 0, VOCAB), jax.random.fold_in(arg_keys[13], 1), 0, VOCAB - 1).astype(jnp.int32)
    return {"qkv_master": qkv_master, "qkv_first": qkv_first, "qkv_second": qkv_second, "qkv_grad": qkv_grad, "out_master": out_master, "out_first": out_first, "out_second": out_second, "out_grad": out_grad, "norm_gain": norm_gain, "embed_table": embed_table, "cache_keys": cache_keys, "cache_values": cache_values, "cache_lengths": cache_lengths, "token_ids": token_ids}


BETA_ONE = 0.9
BETA_TWO = 0.95
LEARN_RATE = 0.004
WEIGHT_DECAY = 0.1
EPS_ADAM = 1e-08
EPS_NORM = 1e-06
CORR_ONE = 1.0 - 0.9 ** 10
CORR_TWO = 1.0 - 0.95 ** 10
MASK_LOW = -1e+30

def adamw(master, first, second, grad):
    gradient = grad.astype(jnp.float32)
    first_new = BETA_ONE * first + (1.0 - BETA_ONE) * gradient
    second_new = BETA_TWO * second + (1.0 - BETA_TWO) * gradient * gradient
    update = first_new / CORR_ONE / (jnp.sqrt(second_new / CORR_TWO) + EPS_ADAM)
    master_new = master - LEARN_RATE * (update + WEIGHT_DECAY * master)
    return (master_new, first_new, second_new)

def attend_row(packed):
    queries, fresh_keys, fresh_values, old_keys, old_values, length = packed
    group_size = HEADS // KV_HEADS
    old_keys32 = old_keys.astype(jnp.float32).reshape(CACHE, KV_HEADS, HEAD)
    old_values32 = old_values.astype(jnp.float32).reshape(CACHE, KV_HEADS, HEAD)
    scale_factor = HEAD ** (-0.5)
    cache_scores = jnp.einsum('sghd,pgd->sghp', queries, old_keys32) * scale_factor
    live = jnp.arange(CACHE, dtype=jnp.int32) < length
    cache_scores = jnp.where(live, cache_scores, MASK_LOW)
    fresh_scores = jnp.einsum('sghd,jgd->sghj', queries, fresh_keys) * scale_factor
    causal = jnp.arange(2, dtype=jnp.int32)[None, :] <= jnp.arange(2, dtype=jnp.int32)[:, None]
    causal = causal[:, None, None, :]
    fresh_scores = jnp.where(causal, fresh_scores, MASK_LOW)
    highest = jnp.maximum(cache_scores.max(-1), fresh_scores.max(-1))
    cache_probs = jnp.where(live, jnp.exp(cache_scores - highest[..., None]), 0.0)
    fresh_probs = jnp.where(causal, jnp.exp(fresh_scores - highest[..., None]), 0.0)
    totals = cache_probs.sum(-1) + fresh_probs.sum(-1)
    weighted = jnp.einsum('sghp,pgd->sghd', cache_probs, old_values32)
    weighted = weighted + jnp.einsum('sghj,jgd->sghd', fresh_probs, fresh_values)
    return (weighted / totals[..., None]).reshape(2, KV_HEADS * group_size * HEAD)

def reference(qkv_master, qkv_first, qkv_second, qkv_grad, out_master, out_first, out_second, out_grad, norm_gain, embed_table, cache_keys, cache_values, cache_lengths, token_ids):
    qkv_master_new, qkv_first_new, qkv_second_new = adamw(qkv_master, qkv_first, qkv_second, qkv_grad)
    out_master_new, out_first_new, out_second_new = adamw(out_master, out_first, out_second, out_grad)
    qkv_weight = qkv_master_new.astype(jnp.bfloat16)
    out_weight = out_master_new.astype(jnp.bfloat16)
    inputs = embed_table[token_ids]
    inputs32 = inputs.astype(jnp.float32)
    meansq = lax.optimization_barrier(jnp.mean(inputs32 * inputs32, axis=-1, keepdims=True))
    normed = (inputs32 * lax.rsqrt(meansq + EPS_NORM) * norm_gain).astype(jnp.bfloat16)
    projected = jnp.dot(normed.reshape(-1, D), qkv_weight, preferred_element_type=jnp.float32)
    projected = projected.astype(jnp.bfloat16).astype(jnp.float32).reshape(ROWS, 2, QKV)
    group_size = HEADS // KV_HEADS
    kv_width = KV_HEADS * HEAD
    queries = projected[..., :D].reshape(ROWS, 2, KV_HEADS, group_size, HEAD)
    fresh_keys = projected[..., D:D + kv_width].reshape(ROWS, 2, KV_HEADS, HEAD)
    fresh_values = projected[..., D + kv_width:].reshape(ROWS, 2, KV_HEADS, HEAD)
    attended = lax.map(attend_row, (queries, fresh_keys, fresh_values, cache_keys, cache_values, cache_lengths))
    attended = attended.astype(jnp.bfloat16)
    mixed = jnp.dot(attended.reshape(-1, D), out_weight, preferred_element_type=jnp.float32).reshape(ROWS, 2, D)
    layer_out = (inputs32 + mixed).astype(jnp.bfloat16)
    return (qkv_master_new, qkv_first_new, qkv_second_new, out_master_new, out_first_new, out_second_new, layer_out)
```

```python
import functools

import jax
import jax.numpy as jnp
from jax import lax
from jax.experimental import pallas as pl
from jax.experimental.pallas import tpu as pltpu
from jax.sharding import PartitionSpec as P

HEADS = 40
KV_HEADS = 8
HEAD = 128
GROUP = HEADS // KV_HEADS
STEPS = 2


BETA_ONE = 0.9
BETA_TWO = 0.95
LEARN_RATE = 0.004
WEIGHT_DECAY = 0.1
EPS_ADAM = 1e-08
EPS_NORM = 1e-06
CORR_ONE = 1.0 - 0.9**10
CORR_TWO = 1.0 - 0.95**10
MASK_LOW = -1e30
BOTH = ("dp", "tp")
F32 = jnp.float32
BF16 = jnp.bfloat16
VMEM_LIMIT = 48 * 1024 * 1024


def adamw(master, first, second, grad):
    gradient = grad.astype(jnp.float32)
    first_new = BETA_ONE * first + (1.0 - BETA_ONE) * gradient
    second_new = BETA_TWO * second + (1.0 - BETA_TWO) * gradient * gradient
    update = first_new / CORR_ONE / (jnp.sqrt(second_new / CORR_TWO) + EPS_ADAM)
    master_new = master - LEARN_RATE * (update + WEIGHT_DECAY * master)
    return (master_new, first_new, second_new)


def lookup_kernel(dp, tp, ids_ref, table_ref, tail_ref, gain_ref, keep_ref, send_ref, own_ref,
                  buf, raw, nrm, sems):
    tokens, width = raw.shape
    vocab_rows = table_ref.shape[0]
    whole = vocab_rows // 16 * 16
    depth = width // (dp * tp)
    my_dp = lax.axis_index("dp")
    base = (my_dp * tp + lax.axis_index("tp")) * vocab_rows

    def local(t):
        return ids_ref[t // STEPS, t % STEPS] - base

    def owned(t):
        entry = local(t)
        return jnp.logical_and(entry >= 0, entry < vocab_rows)

    def fetch(t, _):
        entry = local(t)
        mine = owned(t)

        @pl.when(jnp.logical_and(mine, entry < whole))
        def _():
            start = pl.multiple_of(entry // 16 * 16, 16)
            pltpu.make_async_copy(table_ref.at[pl.ds(start, 16)], buf.at[t], sems.at[t]).start()

        @pl.when(jnp.logical_and(mine, entry >= whole))
        def _():
            pltpu.make_async_copy(tail_ref, buf.at[t], sems.at[t]).start()

        return 0

    lax.fori_loop(0, tokens, fetch, 0)
    raw[...] = jnp.zeros_like(raw)
    nrm[...] = jnp.zeros_like(nrm)

    def take(t, _):
        entry = local(t)

        @pl.when(owned(t))
        def _():
            pltpu.make_async_copy(tail_ref, buf.at[t], sems.at[t]).wait()
            at = jnp.where(entry < whole, entry % 16, entry - (vocab_rows - 16))
            picked = lax.broadcasted_iota(jnp.int32, (16, width), 0) == at
            row = jnp.sum(
                jnp.where(picked, buf[t].astype(F32), 0.0), axis=0, keepdims=True
            )
            meansq = jnp.mean(row * row, axis=-1, keepdims=True)
            raw[pl.ds(t, 1), :] = row
            nrm[pl.ds(t, 1), :] = row * lax.rsqrt(meansq + EPS_NORM) * gain_ref[...]

        return 0

    lax.fori_loop(0, tokens, take, 0)
    own_ref[...] = raw[...].astype(BF16)
    quarter = tokens // 4

    def block(b):
        main = nrm[:, depth * b : depth * b + 128]
        rest = nrm[:, depth * b + 128 : depth * (b + 1)]
        rest = jnp.concatenate(
            [rest[quarter * i : quarter * (i + 1)] for i in range(4)], axis=1
        )
        return jnp.concatenate([main, rest], axis=0)

    even = my_dp % 2 == 0
    for x in range(dp // 2):
        for t in range(tp):
            at_even = block((2 * x) * tp + t)
            at_odd = block((2 * x + 1) * tp + t)
            keep_ref[x * tp + t] = jnp.where(even, at_even, at_odd).astype(BF16)
            send_ref[x * tp + t] = jnp.where(even, at_odd, at_even).astype(BF16)


def by_core(rows, dp, per_dp):
    even = lax.axis_index("dp") % 2 == 0
    mine, other = [], []
    for x in range(dp // 2):
        at_even = rows[(2 * x) * per_dp : (2 * x + 1) * per_dp]
        at_odd = rows[(2 * x + 1) * per_dp : (2 * x + 2) * per_dp]
        mine.append(jnp.where(even, at_even, at_odd))
        other.append(jnp.where(even, at_odd, at_even))
    return jnp.concatenate(mine + other, axis=0)


def project_kernel(dp, tp, blocks_ref, weight_ref, keep_ref, send_ref):
    tokens = 64
    per_dp = tokens // dp
    quarter = tokens // 4
    width = HEADS * HEAD
    kv_width = KV_HEADS * HEAD
    total = jnp.sum(blocks_ref[...].astype(F32), axis=0)
    main = by_core(total[:tokens], dp, per_dp).astype(BF16)
    rest = total[tokens:]
    rest = jnp.concatenate([rest[:, 32 * i : 32 * (i + 1)] for i in range(4)], axis=0)
    rest = by_core(rest, dp, per_dp).astype(BF16)
    half = tokens // 2

    def dot(at, size):
        return jnp.dot(
            main, weight_ref[0:128, at : at + size], preferred_element_type=F32
        ) + jnp.dot(rest, weight_ref[128:160, at : at + size], preferred_element_type=F32)

    for g in range(tp):
        spans = (
            (0, g * GROUP * HEAD, GROUP * HEAD),
            (GROUP * HEAD, width + g * HEAD, HEAD),
            ((GROUP + 1) * HEAD, width + kv_width + g * HEAD, HEAD),
        )
        for to, at, size in spans:
            part = dot(at, size)
            for x in range(dp // 2):
                keep_ref[x * tp + g, :, to : to + size] = part[per_dp * x : per_dp * (x + 1)]
                send_ref[x * tp + g, :, to : to + size] = part[
                    half + per_dp * x : half + per_dp * (x + 1)
                ]


def attend_kernel(dp, tp, lengths_ref, qkv_ref, keys_ref, values_ref, msg_ref, joined, level):
    g = pl.program_id(0)
    rows, span = keys_ref.shape[0], keys_ref.shape[1]
    per_dp = rows * STEPS
    lines = GROUP * per_dp
    my_tp = lax.axis_index("tp")
    depth = HEADS * HEAD // (dp * tp)
    scale = HEAD ** (-0.5)

    packed = qkv_ref[0]
    queries = jnp.concatenate(
        [packed[:, HEAD * h : HEAD * (h + 1)] for h in range(GROUP)], axis=0
    )
    fresh_keys = packed[:, GROUP * HEAD : (GROUP + 1) * HEAD]
    fresh_values = packed[:, (GROUP + 1) * HEAD :]
    nt = (((1,), (1,)), ((), ()))

    line = lax.broadcasted_iota(jnp.int32, (lines, 1), 0) % per_dp
    row_of = line // STEPS
    length = jnp.zeros((lines, 1), jnp.int32)
    scores = jnp.zeros((lines, span), F32)
    for r in range(rows):
        length = jnp.where(row_of == r, lengths_ref[r], length)
        part = lax.dot_general(queries, keys_ref[r], nt, preferred_element_type=F32)
        scores = jnp.where(row_of == r, part, scores)
    position = my_tp * span + lax.broadcasted_iota(jnp.int32, (lines, span), 1)
    live = position < length
    scores = jnp.where(live, scores * scale, MASK_LOW)

    column = lax.broadcasted_iota(jnp.int32, (lines, per_dp), 1)
    fresh = lax.dot_general(queries, fresh_keys, nt, preferred_element_type=F32) * scale
    seen = (column // STEPS == row_of) & (column <= line) & (my_tp == g)
    fresh = jnp.where(seen, fresh, MASK_LOW)

    top = jnp.maximum(
        jnp.max(scores, axis=-1, keepdims=True), jnp.max(fresh, axis=-1, keepdims=True)
    )
    probs = jnp.where(live, jnp.exp(scores - top), 0.0)
    fresh_probs = jnp.where(seen, jnp.exp(fresh - top), 0.0)
    total = jnp.sum(probs, axis=-1, keepdims=True) + jnp.sum(fresh_probs, axis=-1, keepdims=True)
    weighted = jnp.dot(fresh_probs.astype(BF16), fresh_values, preferred_element_type=F32)
    probs = probs.astype(BF16)
    for r in range(rows):
        weighted += jnp.dot(
            jnp.where(row_of == r, probs, jnp.zeros_like(probs)),
            values_ref[r],
            preferred_element_type=F32,
        )
    some = total > 0.0
    safe = jnp.where(some, total, 1.0)
    outcome = weighted / safe
    logsum = jnp.where(some, top + jnp.log(safe), MASK_LOW)
    lane = lax.broadcasted_iota(jnp.int32, (per_dp, HEAD), 1)
    levels = level[...]
    for h in range(GROUP):
        at = pl.multiple_of((g * GROUP + h) * HEAD, HEAD)
        joined[:, pl.ds(at, HEAD)] = outcome[per_dp * h : per_dp * (h + 1)]
        levels = jnp.where(
            lane == g * GROUP + h, logsum[per_dp * h : per_dp * (h + 1)], levels
        )
    level[...] = levels

    @pl.when(g == KV_HEADS - 1)
    def _():
        final = level[...]
        high = final.astype(BF16).astype(F32)
        middle = (final - high).astype(BF16).astype(F32)
        low = final - high - middle
        for b in range(dp * tp):
            h = depth * b // HEAD
            pieces = [joined[:, depth * b : depth * (b + 1)]]
            for head in (h, h + 1):
                for part in (high, middle, low):
                    pieces.append(part[:, head : head + 1])
            pieces.append(jnp.zeros((per_dp, 256 - depth - 6), F32))
            msg_ref[b] = jnp.concatenate(pieces, axis=1).astype(BF16)


def output_kernel(dp, tp, msg_ref, weight_ref, own_ref, keep_ref, send_ref):
    depth = weight_ref.shape[0]
    per_dp = msg_ref.shape[1]
    my_block = lax.axis_index("dp") * tp + lax.axis_index("tp")
    edge = HEAD - (depth * my_block) % HEAD
    first_head = lax.broadcasted_iota(jnp.int32, (per_dp, depth), 1) < edge
    merged = []
    for d in range(dp):
        parts, levels = [], []
        for t in range(tp):
            block = msg_ref[d * tp + t].astype(F32)
            stats = [block[:, depth + i : depth + i + 1] for i in range(6)]
            one = stats[0] + stats[1] + stats[2]
            two = stats[3] + stats[4] + stats[5]
            levels.append(jnp.where(first_head, one, two))
            parts.append(block[:, :depth])
        top = functools.reduce(jnp.maximum, levels)
        total = jnp.zeros_like(top)
        weighted = jnp.zeros_like(top)
        for part, lev in zip(parts, levels):
            share = jnp.exp(lev - top)
            total += share
            weighted += share * part
        merged.append(weighted / total)
    attended = by_core(jnp.concatenate(merged, axis=0), dp, per_dp).astype(BF16)
    half = dp // 2 * per_dp
    out_width = weight_ref.shape[1] // tp
    for t in range(tp):
        cols = slice(out_width * t, out_width * (t + 1))
        part = jnp.dot(attended, weight_ref[:, cols], preferred_element_type=F32)
        part += by_core(own_ref[:, cols].astype(F32), dp, per_dp)
        for x in range(dp // 2):
            keep_ref[x * tp + t] = part[per_dp * x : per_dp * (x + 1)]
            send_ref[x * tp + t] = part[half + per_dp * x : half + per_dp * (x + 1)]


def whole(shape_count):
    return [pl.BlockSpec(memory_space=pltpu.VMEM)] * shape_count


def on_device_partial(
    dp,
    tp,
    qkv_master,
    qkv_first,
    qkv_second,
    qkv_grad,
    out_master,
    out_first,
    out_second,
    out_grad,
    norm_gain,
    embed_table,
    cache_keys,
    cache_values,
    cache_lengths,
    token_ids,
):
    width = embed_table.shape[1]
    group_rows, span = cache_keys.shape[0], cache_keys.shape[1]
    per_dp = group_rows * STEPS
    tokens = per_dp * dp
    half = dp // 2 * tp
    depth = width // (dp * tp)
    packed = width // (dp * tp) * tokens // 128
    out_width = width // tp
    joined_width = (GROUP + 2) * HEAD
    params = pltpu.CompilerParams(vmem_limit_bytes=VMEM_LIMIT)

    core_pairs = [
        (d * tp + t, (d ^ 1) * tp + t) for d in range(dp) for t in range(tp)
    ]
    same_core = [
        [(2 * x + c) * tp + t for x in range(dp // 2) for t in range(tp)] for c in range(2)
    ]

    def other_core(value):
        return lax.ppermute(value, BOTH, core_pairs)

    def among_chips(value):
        return lax.all_to_all(value, BOTH, 0, 0, tiled=True, axis_index_groups=same_core)

    keep, send, own_rows = pl.pallas_call(
        functools.partial(lookup_kernel, dp, tp),
        out_shape=(
            jax.ShapeDtypeStruct((half, packed, 128), BF16),
            jax.ShapeDtypeStruct((half, packed, 128), BF16),
            jax.ShapeDtypeStruct((tokens, width), BF16),
        ),
        in_specs=[
            pl.BlockSpec(memory_space=pltpu.SMEM),
            pl.BlockSpec(memory_space=pl.ANY),
            pl.BlockSpec(memory_space=pl.ANY),
            pl.BlockSpec(memory_space=pltpu.VMEM),
        ],
        out_specs=tuple(whole(3)),
        scratch_shapes=[
            pltpu.VMEM((tokens, 16, width), BF16),
            pltpu.VMEM((tokens, width), F32),
            pltpu.VMEM((tokens, width), F32),
            pltpu.SemaphoreType.DMA((tokens,)),
        ],
        compiler_params=params,
        name="lookup",
    )(token_ids, embed_table, embed_table[-16:], norm_gain.reshape(1, width))
    blocks = among_chips(keep + other_core(send))

    qkv_master_new, qkv_first_new, qkv_second_new = adamw(
        qkv_master, qkv_first, qkv_second, qkv_grad
    )
    out_master_new, out_first_new, out_second_new = adamw(
        out_master, out_first, out_second, out_grad
    )
    qkv_half = qkv_master_new.astype(BF16)
    out_half = out_master_new.astype(BF16)

    keep, send = pl.pallas_call(
        functools.partial(project_kernel, dp, tp),
        out_shape=(jax.ShapeDtypeStruct((half, per_dp, joined_width), F32),) * 2,
        in_specs=whole(2),
        out_specs=tuple(whole(2)),
        compiler_params=params,
        name="project",
    )(blocks, qkv_half)
    partial = among_chips(keep + other_core(send))
    projected = jnp.sum(partial, axis=0).astype(BF16)
    joined = lax.all_to_all(
        jnp.broadcast_to(projected[None], (tp,) + projected.shape), "tp", 0, 0, tiled=True
    )

    messages = pl.pallas_call(
        functools.partial(attend_kernel, dp, tp),
        grid=(KV_HEADS,),
        out_shape=jax.ShapeDtypeStruct((dp * tp, per_dp, 256), BF16),
        in_specs=[
            pl.BlockSpec(memory_space=pltpu.SMEM),
            pl.BlockSpec((1, per_dp, joined_width), lambda g: (g, 0, 0)),
            pl.BlockSpec((group_rows, span, HEAD), lambda g: (0, 0, g)),
            pl.BlockSpec((group_rows, span, HEAD), lambda g: (0, 0, g)),
        ],
        out_specs=pl.BlockSpec((dp * tp, per_dp, 256), lambda g: (0, 0, 0)),
        scratch_shapes=[pltpu.VMEM((per_dp, width), F32), pltpu.VMEM((per_dp, HEAD), F32)],
        compiler_params=params,
        name="attend",
    )(cache_lengths, joined, cache_keys, cache_values)
    arrived = lax.all_to_all(messages, BOTH, 0, 0, tiled=True)

    keep, send = pl.pallas_call(
        functools.partial(output_kernel, dp, tp),
        out_shape=(jax.ShapeDtypeStruct((half, per_dp, out_width), F32),) * 2,
        in_specs=whole(3),
        out_specs=tuple(whole(2)),
        compiler_params=params,
        name="output",
    )(arrived, out_half, own_rows)
    sums = among_chips((keep + other_core(send)).astype(BF16))
    layer_out = jnp.sum(sums.astype(F32), axis=0).astype(BF16)
    return (
        qkv_master_new,
        qkv_first_new,
        qkv_second_new,
        out_master_new,
        out_first_new,
        out_second_new,
        layer_out.reshape(group_rows, STEPS, out_width),
    )


def on_device_general(
    qkv_master,
    qkv_first,
    qkv_second,
    qkv_grad,
    out_master,
    out_first,
    out_second,
    out_grad,
    norm_gain,
    embed_table,
    cache_keys,
    cache_values,
    cache_lengths,
    token_ids,
):
    qkv_master_new, qkv_first_new, qkv_second_new = adamw(
        qkv_master, qkv_first, qkv_second, qkv_grad
    )
    out_master_new, out_first_new, out_second_new = adamw(
        out_master, out_first, out_second, out_grad
    )
    qkv_half = qkv_master_new.astype(jnp.bfloat16)
    out_half = out_master_new.astype(jnp.bfloat16)
    qkv_group, out_group = (
        lax.all_to_all(qkv_half, "tp", split_axis=1, concat_axis=0, tiled=True),
        lax.all_to_all(out_half, "tp", split_axis=1, concat_axis=0, tiled=True),
    )
    qkv_cols, out_cols = (
        lax.all_gather(qkv_group, "dp", axis=0, tiled=True),
        lax.all_gather(out_group, "dp", axis=0, tiled=True),
    )
    width = embed_table.shape[1]
    vocab_rows = embed_table.shape[0]
    group_rows = cache_keys.shape[0]
    first_entry = lax.axis_index(("dp", "tp")) * vocab_rows
    local_ids = token_ids.reshape(-1) - first_entry
    selector = (local_ids[:, None] == jnp.arange(vocab_rows, dtype=jnp.int32)[None, :]).astype(
        jnp.bfloat16
    )
    partial_rows = jnp.dot(selector, embed_table, preferred_element_type=jnp.float32).reshape(
        -1, 2, width
    )
    every_row = lax.psum(partial_rows, ("dp", "tp"))
    own_inputs = lax.dynamic_slice_in_dim(
        every_row, lax.axis_index("dp") * group_rows, group_rows, 0
    )
    meansq = jnp.mean(own_inputs * own_inputs, axis=-1, keepdims=True)
    normed = (own_inputs * lax.rsqrt(meansq + EPS_NORM) * norm_gain).astype(jnp.bfloat16)
    proj_part = jnp.dot(
        normed.reshape(-1, width), qkv_cols, preferred_element_type=jnp.float32
    ).astype(jnp.bfloat16)
    projected = lax.all_gather(proj_part, "tp", axis=1, tiled=True).reshape(group_rows, 2, -1)
    group_size = HEADS // KV_HEADS
    kv_width = KV_HEADS * HEAD
    scale_factor = HEAD ** (-0.5)
    queries = projected[..., :width].reshape(group_rows, 2, KV_HEADS, group_size, HEAD)
    fresh_keys = projected[..., width : width + kv_width].reshape(group_rows, 2, KV_HEADS, HEAD)
    fresh_values = projected[..., width + kv_width :].reshape(group_rows, 2, KV_HEADS, HEAD)
    span = cache_keys.shape[1]
    old_keys = cache_keys.reshape(group_rows, span, KV_HEADS, HEAD)
    old_values = cache_values.reshape(group_rows, span, KV_HEADS, HEAD)
    cache_scores = (
        jnp.einsum("rsghd,rpgd->rsghp", queries, old_keys, preferred_element_type=jnp.float32)
        * scale_factor
    )
    position = lax.axis_index("tp") * span + jnp.arange(span, dtype=jnp.int32)
    live = (position[None, :] < cache_lengths[:, None])[:, None, None, None, :]
    cache_scores = jnp.where(live, cache_scores, MASK_LOW)
    local_top = cache_scores.max(-1)
    cache_probs = jnp.where(live, jnp.exp(cache_scores - local_top[..., None]), 0.0)
    local_total = cache_probs.sum(-1)
    local_weighted = jnp.einsum(
        "rsghp,rpgd->rsghd", cache_probs, old_values, preferred_element_type=jnp.float32
    )
    cache_top = lax.pmax(local_top, "tp")
    rescale = jnp.exp(local_top - cache_top)
    cache_total, cache_weighted = lax.psum(
        (local_total * rescale, local_weighted * rescale[..., None]), "tp"
    )
    fresh_scores = (
        jnp.einsum("rsghd,rjgd->rsghj", queries, fresh_keys, preferred_element_type=jnp.float32)
        * scale_factor
    )
    causal = jnp.arange(2, dtype=jnp.int32)[None, :] <= jnp.arange(2, dtype=jnp.int32)[:, None]
    causal = causal[None, :, None, None, :]
    fresh_scores = jnp.where(causal, fresh_scores, MASK_LOW)
    highest = jnp.maximum(cache_top, fresh_scores.max(-1))
    cache_scale = jnp.exp(cache_top - highest)
    fresh_probs = jnp.where(causal, jnp.exp(fresh_scores - highest[..., None]), 0.0)
    totals = cache_total * cache_scale + fresh_probs.sum(-1)
    weighted = cache_weighted * cache_scale[..., None]
    weighted = weighted + jnp.einsum(
        "rsghj,rjgd->rsghd", fresh_probs, fresh_values.astype(jnp.float32)
    )
    attended = (weighted / totals[..., None]).reshape(group_rows * 2, width).astype(jnp.bfloat16)
    out_width = out_cols.shape[1]
    mixed = jnp.dot(attended, out_cols, preferred_element_type=jnp.float32).reshape(
        group_rows, 2, out_width
    )
    residual_cols = lax.dynamic_slice_in_dim(
        own_inputs, lax.axis_index("tp") * out_width, out_width, 2
    )
    layer_out = (residual_cols + mixed).astype(jnp.bfloat16)
    return (
        qkv_master_new,
        qkv_first_new,
        qkv_second_new,
        out_master_new,
        out_first_new,
        out_second_new,
        layer_out,
    )


def solution(mesh):
    dp, tp = mesh.shape["dp"], mesh.shape["tp"]
    placed = (
        P(("dp", "tp"), None),
        P(("dp", "tp"), None),
        P(("dp", "tp"), None),
        P(("dp", "tp"), None),
        P(("dp", "tp"), None),
        P(("dp", "tp"), None),
        P(("dp", "tp"), None),
        P(("dp", "tp"), None),
        P(),
        P(("dp", "tp"), None),
        P("dp", "tp", None),
        P("dp", "tp", None),
        P("dp"),
        P(),
    )
    body = on_device_general
    if (dp, tp) == (4, KV_HEADS):
        body = functools.partial(on_device_partial, dp, tp)
    return jax.shard_map(
        body,
        mesh=mesh,
        in_specs=placed,
        out_specs=(
            P(("dp", "tp"), None),
            P(("dp", "tp"), None),
            P(("dp", "tp"), None),
            P(("dp", "tp"), None),
            P(("dp", "tp"), None),
            P(("dp", "tp"), None),
            P("dp", None, "tp"),
        ),
        check_vma=False,
    )
```

```python
import functools

import jax
import jax.numpy as jnp
from jax import lax
from jax.experimental import pallas as pl
from jax.experimental.pallas import tpu as pltpu
from jax.sharding import PartitionSpec as P

HEADS = 40
KV_HEADS = 8
HEAD = 128
GROUP = HEADS // KV_HEADS
STEPS = 2
SLOTS = 8


BETA_ONE = 0.9
BETA_TWO = 0.95
LEARN_RATE = 0.004
WEIGHT_DECAY = 0.1
EPS_ADAM = 1e-08
EPS_NORM = 1e-06
CORR_ONE = 1.0 - 0.9**10
CORR_TWO = 1.0 - 0.95**10
MASK_LOW = -1e30
BOTH = ("dp", "tp")
F32 = jnp.float32
BF16 = jnp.bfloat16
MIB = 1024 * 1024


def adamw(master, first, second, grad):
    gradient = grad.astype(jnp.float32)
    first_new = BETA_ONE * first + (1.0 - BETA_ONE) * gradient
    second_new = BETA_TWO * second + (1.0 - BETA_TWO) * gradient * gradient
    update = first_new / CORR_ONE / (jnp.sqrt(second_new / CORR_TWO) + EPS_ADAM)
    master_new = master - LEARN_RATE * (update + WEIGHT_DECAY * master)
    return (master_new, first_new, second_new)


def lookup_kernel(dp, tp, ids_ref, table_ref, gain_ref, msg_ref, raw_ref, place_ref, most_ref,
                  buf, gain, raw, column, entries, sems, gain_sem):
    tokens, width = raw.shape
    per_dp = tokens // dp
    vocab_rows = table_ref.shape[0]
    whole = vocab_rows // 16 * 16
    left = vocab_rows - whole
    depth = width // (dp * tp)
    my_core = lax.axis_index("dp") % 2
    base = (lax.axis_index("dp") * tp + lax.axis_index("tp")) * vocab_rows
    gain_copy = pltpu.make_async_copy(gain_ref, gain, gain_sem)
    gain_copy.start()

    def whole_rows(entry, rank):
        start = pl.multiple_of(entry // 16 * 16, 16)
        return pltpu.make_async_copy(
            table_ref.at[pl.ds(start, 16)], buf.at[rank], sems.at[rank]
        )

    def last_rows(rank):
        return pltpu.make_async_copy(
            table_ref.at[pl.ds(whole, left)], buf.at[rank, pl.ds(0, left)], sems.at[rank]
        )

    def fetch(t, held):
        entry = ids_ref[t % STEPS, t // STEPS] - base
        mine = jnp.logical_and(entry >= 0, entry < vocab_rows)
        entries[held] = entry

        @pl.when(jnp.logical_and(mine, entry < whole))
        def _():
            whole_rows(entry, held).start()

        if left:
            @pl.when(jnp.logical_and(mine, entry >= whole))
            def _():
                last_rows(held).start()

        return held + mine.astype(jnp.int32)

    buf[0:SLOTS] = jnp.zeros((SLOTS, 16, width), BF16)
    held = lax.fori_loop(0, tokens, fetch, 0)
    raw_ref[SLOTS:] = jnp.zeros((tokens - SLOTS, width), BF16)

    def write(t, _):
        group = t // per_dp
        line = (group % 2 ^ my_core) * (tokens // 2) + group // 2 * per_dp + t % per_dp
        column[pl.ds(line, 1), :] = jnp.full(
            (1, 128), ids_ref[t % STEPS, t // STEPS], jnp.int32
        )
        return 0

    lax.fori_loop(0, tokens, write, 0, unroll=8)
    line = lax.broadcasted_iota(jnp.int32, (tokens, 128), 0)
    inside = line % (tokens // 2)
    order = (inside // per_dp * 2 + (line // (tokens // 2) ^ my_core)) * per_dp + line % per_dp
    identity = column[...].astype(F32)
    holder = jnp.floor(identity * (1.0 / vocab_rows))
    holder = jnp.where(holder * vocab_rows > identity, holder - 1.0, holder)
    holder = jnp.where((holder + 1.0) * vocab_rows <= identity, holder + 1.0, holder)
    key = holder * tokens + order.astype(F32)
    turned = jnp.transpose(
        jnp.concatenate([key, jnp.full((128 - tokens, 128), -1.0, F32)], axis=0)
    )[0:1, :]
    before = (turned >= holder * tokens) & (turned < key)
    rank = jnp.sum(before.astype(F32), axis=1, keepdims=True)
    place_ref[...] = (holder * tokens + rank).astype(jnp.int32)
    most_ref[0] = jnp.max(rank).astype(jnp.int32)

    def arrive(rank):
        entry = entries[rank]

        @pl.when(entry < whole)
        def _():
            whole_rows(entry, rank).wait()

        if left:
            @pl.when(entry >= whole)
            def _():
                last_rows(rank).wait()

        return entry % 16

    source = jnp.full((SLOTS, 1), -1, jnp.int32)
    slot = lax.broadcasted_iota(jnp.int32, (SLOTS, 1), 0)
    for rank in range(SLOTS):
        @pl.when(rank < held)
        def _():
            arrive(rank)

        at = jnp.where(rank < held, rank * 16 + entries[rank] % 16, -1)
        source = jnp.where(slot == rank, at, source)
    select = (
        lax.broadcasted_iota(jnp.int32, (SLOTS, SLOTS * 16), 1) == source
    ).astype(BF16)
    rows = jnp.dot(
        select, buf[0:SLOTS].reshape(SLOTS * 16, width), preferred_element_type=F32
    )
    gain_copy.wait()
    scale = lax.rsqrt(jnp.mean(rows * rows, axis=-1, keepdims=True) + EPS_NORM)
    first = rows * scale * gain[...]
    for b in range(dp * tp):
        rest = jnp.concatenate(
            [
                first[:, depth * b + 128 : depth * (b + 1)],
                jnp.zeros((SLOTS, 256 - depth), F32),
            ],
            axis=1,
        )
        msg_ref[b] = jnp.concatenate(
            [first[:, depth * b : depth * b + 128], rest], axis=0
        ).astype(BF16)
    raw_ref[0:SLOTS] = rows.astype(BF16)

    @pl.when(held > SLOTS)
    def _():
        raw[...] = jnp.zeros_like(raw)
        raw[0:SLOTS] = rows

        def take(rank, _):
            picked = lax.broadcasted_iota(jnp.int32, (16, width), 0) == arrive(rank)
            raw[pl.ds(rank, 1), :] = jnp.sum(
                jnp.where(picked, buf[rank].astype(F32), 0.0), axis=0, keepdims=True
            )
            return 0

        lax.fori_loop(SLOTS, held, take, 0)
        raw_ref[...] = raw[...].astype(BF16)


def by_core(rows, dp, per_dp):
    even = lax.axis_index("dp") % 2 == 0
    mine, other = [], []
    for x in range(dp // 2):
        at_even = rows[(2 * x) * per_dp : (2 * x + 1) * per_dp]
        at_odd = rows[(2 * x + 1) * per_dp : (2 * x + 2) * per_dp]
        mine.append(jnp.where(even, at_even, at_odd))
        other.append(jnp.where(even, at_odd, at_even))
    return jnp.concatenate(mine + other, axis=0)


def project_kernel(dp, tp, place_ref, msg_ref, extra_ref, weight_ref, keep_ref, send_ref):
    tokens = place_ref.shape[0]
    per_dp = tokens // dp
    width = HEADS * HEAD
    kv_width = KV_HEADS * HEAD
    slots = dp * tp * SLOTS
    blocks = msg_ref[...].astype(F32)
    place = place_ref[:, 0:1]
    holder, rank = place // tokens, place % tokens
    place = jnp.where(rank < SLOTS, holder * SLOTS + rank, -1)
    select = (lax.broadcasted_iota(jnp.int32, (tokens, slots), 1) == place).astype(BF16)
    extra = extra_ref[...].astype(F32)

    def pick(rows, more):
        rows = rows.reshape(slots, 128).astype(BF16)
        return (jnp.dot(select, rows, preferred_element_type=F32) + more).astype(BF16)

    main = pick(blocks[:, :SLOTS], extra[:, :128])
    rest = pick(blocks[:, SLOTS:], extra[:, 128:])[:, : weight_ref.shape[0] - 128]
    half = tokens // 2

    def dot(at, size):
        return jnp.dot(
            main, weight_ref[0:128, at : at + size], preferred_element_type=F32
        ) + jnp.dot(rest, weight_ref[128:, at : at + size], preferred_element_type=F32)

    for g in range(tp):
        spans = (
            (0, g * GROUP * HEAD, GROUP * HEAD),
            (GROUP * HEAD, width + g * HEAD, HEAD),
            ((GROUP + 1) * HEAD, width + kv_width + g * HEAD, HEAD),
        )
        for to, at, size in spans:
            part = dot(at, size)
            for x in range(dp // 2):
                keep_ref[x * tp + g, :, to : to + size] = part[per_dp * x : per_dp * (x + 1)]
                send_ref[x * tp + g, :, to : to + size] = part[
                    half + per_dp * x : half + per_dp * (x + 1)
                ]


def attend_kernel(dp, tp, lengths_ref, qkv_ref, keys_ref, values_ref, msg_ref,
                  keys, values, scores_of, probs_of, weighted_of, joined, key_sems, value_sems):
    rows, span = keys.shape[0], keys.shape[1]
    per_dp = rows * STEPS
    lines = GROUP * per_dp
    my_tp = lax.axis_index("tp")
    depth = HEADS * HEAD // (dp * tp)
    scale = HEAD ** (-0.5)
    nt = (((1,), (1,)), ((), ()))

    def copies(source, target, sems):
        return [
            pltpu.make_async_copy(source.at[r], target.at[r], sems.at[r]) for r in range(rows)
        ]

    key_copies = copies(keys_ref, keys, key_sems)
    value_copies = copies(values_ref, values, value_sems)
    for copy in key_copies + value_copies:
        copy.start()

    line = lax.broadcasted_iota(jnp.int32, (lines, 1), 0) % per_dp
    row_of = line // STEPS
    length = jnp.zeros((lines, 1), jnp.int32)
    for r in range(rows):
        length = jnp.where(row_of == r, lengths_ref[r], length)
    position = my_tp * span + lax.broadcasted_iota(jnp.int32, (lines, span), 1)
    live = position < length
    column = lax.broadcasted_iota(jnp.int32, (lines, per_dp), 1)
    causal = (column // STEPS == row_of) & (column <= line)

    queries = []
    for g in range(KV_HEADS):
        queries.append(
            jnp.concatenate(
                [qkv_ref[g, :, HEAD * h : HEAD * (h + 1)] for h in range(GROUP)], axis=0
            )
        )
    for r in range(rows):
        key_copies[r].wait()
        for g in range(KV_HEADS):
            part = lax.dot_general(
                queries[g],
                keys[r, :, HEAD * g : HEAD * (g + 1)],
                nt,
                preferred_element_type=F32,
            )
            scores_of[g] = part if r == 0 else jnp.where(row_of == r, part, scores_of[g])
    kept = []
    for g in range(KV_HEADS):
        fresh_keys = qkv_ref[g, :, GROUP * HEAD : (GROUP + 1) * HEAD]
        fresh_values = qkv_ref[g, :, (GROUP + 1) * HEAD :]
        scores = jnp.where(live, scores_of[g] * scale, MASK_LOW)
        fresh = lax.dot_general(queries[g], fresh_keys, nt, preferred_element_type=F32) * scale
        seen = causal & (my_tp == g)
        fresh = jnp.where(seen, fresh, MASK_LOW)
        top = jnp.maximum(
            jnp.max(scores, axis=-1, keepdims=True), jnp.max(fresh, axis=-1, keepdims=True)
        )
        probs = jnp.where(live, jnp.exp(scores - top), 0.0)
        fresh_probs = jnp.where(seen, jnp.exp(fresh - top), 0.0)
        total = jnp.sum(probs, axis=-1, keepdims=True)
        total += jnp.sum(fresh_probs, axis=-1, keepdims=True)
        probs_of[g] = probs.astype(BF16)
        weighted_of[g] = jnp.dot(
            fresh_probs.astype(BF16), fresh_values, preferred_element_type=F32
        )
        kept.append((top, total))
    for r in range(rows):
        value_copies[r].wait()
        for g in range(KV_HEADS):
            probs = probs_of[g]
            weighted_of[g] += jnp.dot(
                jnp.where(row_of == r, probs, jnp.zeros_like(probs)),
                values[r, :, HEAD * g : HEAD * (g + 1)],
                preferred_element_type=F32,
            )

    lane = lax.broadcasted_iota(jnp.int32, (per_dp, HEAD), 1)
    levels = jnp.zeros((per_dp, HEAD), F32)
    for g in range(KV_HEADS):
        top, total = kept[g]
        some = total > 0.0
        safe = jnp.where(some, total, 1.0)
        outcome = weighted_of[g] / safe
        logsum = jnp.where(some, top + jnp.log(safe), MASK_LOW)
        for h in range(GROUP):
            head = g * GROUP + h
            joined[:, HEAD * head : HEAD * (head + 1)] = outcome[per_dp * h : per_dp * (h + 1)]
            one = logsum[per_dp * h : per_dp * (h + 1)]
            high = one.astype(BF16).astype(F32)
            middle = (one - high).astype(BF16).astype(F32)
            for i, part in enumerate((high, middle, one - high - middle)):
                levels = jnp.where(lane == 3 * head + i, part, levels)
    for b in range(dp * tp):
        at = depth * b
        turned = pltpu.roll(levels, (depth - 128 - 3 * (at // HEAD)) % 128, 1)
        rest = jnp.concatenate(
            [joined[:, at + 128 : at + depth], jnp.zeros((per_dp, 256 - depth), F32)], axis=1
        )
        rest = jnp.where(lane < depth - 128, rest, turned)
        msg_ref[b] = jnp.concatenate([joined[:, at : at + 128], rest], axis=1).astype(BF16)


def output_kernel(dp, tp, place_ref, msg_ref, weight_ref, raw_ref, keep_ref, send_ref):
    depth = weight_ref.shape[0]
    tokens, per_dp = place_ref.shape[0], msg_ref.shape[1]
    my_block = lax.axis_index("dp") * tp + lax.axis_index("tp")
    edge = HEAD - (depth * my_block) % HEAD
    first_head = lax.broadcasted_iota(jnp.int32, (per_dp, depth), 1) < edge
    merged = []
    for d in range(dp):
        parts, levels = [], []
        for t in range(tp):
            block = msg_ref[d * tp + t].astype(F32)
            stats = [block[:, depth + i : depth + i + 1] for i in range(6)]
            one = stats[0] + stats[1] + stats[2]
            two = stats[3] + stats[4] + stats[5]
            levels.append(jnp.where(first_head, one, two))
            parts.append(block[:, :depth])
        top = functools.reduce(jnp.maximum, levels)
        total = jnp.zeros_like(top)
        weighted = jnp.zeros_like(top)
        for part, lev in zip(parts, levels):
            share = jnp.exp(lev - top)
            total += share
            weighted += share * part
        merged.append(weighted / total)
    attended = by_core(jnp.concatenate(merged, axis=0), dp, per_dp).astype(BF16)
    place = place_ref[:, 0:1] - my_block * tokens
    select = (lax.broadcasted_iota(jnp.int32, (tokens, tokens), 1) == place).astype(BF16)
    half = tokens // 2
    out_width = weight_ref.shape[1] // tp
    for t in range(tp):
        cols = slice(out_width * t, out_width * (t + 1))
        part = jnp.dot(attended, weight_ref[:, cols], preferred_element_type=F32)
        part += jnp.dot(select, raw_ref[:, cols], preferred_element_type=F32)
        for x in range(dp // 2):
            keep_ref[x * tp + t] = part[per_dp * x : per_dp * (x + 1)]
            send_ref[x * tp + t] = part[half + per_dp * x : half + per_dp * (x + 1)]


def finish_kernel(sums_ref, out_ref):
    total = jnp.sum(sums_ref[...].astype(F32), axis=0)
    out_ref[...] = total.reshape(out_ref.shape).astype(BF16)


def whole(shape_count):
    return [pl.BlockSpec(memory_space=pltpu.VMEM)] * shape_count


def on_device_partial(
    dp,
    tp,
    qkv_master,
    qkv_first,
    qkv_second,
    qkv_grad,
    out_master,
    out_first,
    out_second,
    out_grad,
    norm_gain,
    embed_table,
    cache_keys,
    cache_values,
    cache_lengths,
    token_ids,
):
    width = embed_table.shape[1]
    group_rows, span = cache_keys.shape[0], cache_keys.shape[1]
    per_dp = group_rows * STEPS
    tokens = per_dp * dp
    half = dp // 2 * tp
    depth = width // (dp * tp)
    out_width = width // tp
    joined_width = (GROUP + 2) * HEAD

    def granted(size):
        return pltpu.CompilerParams(vmem_limit_bytes=size * MIB)


    core_pairs = [
        (d * tp + t, (d ^ 1) * tp + t) for d in range(dp) for t in range(tp)
    ]
    same_core = [
        [(2 * x + c) * tp + t for x in range(dp // 2) for t in range(tp)] for c in range(2)
    ]

    def other_core(value):
        return lax.ppermute(value, BOTH, core_pairs)

    def among_chips(value):
        return lax.all_to_all(value, BOTH, 0, 0, tiled=True, axis_index_groups=same_core)

    message, raw_rows, place, most = pl.pallas_call(
        functools.partial(lookup_kernel, dp, tp),
        out_shape=(
            jax.ShapeDtypeStruct((dp * tp, 2 * SLOTS, 128), BF16),
            jax.ShapeDtypeStruct((tokens, width), BF16),
            jax.ShapeDtypeStruct((tokens, 128), jnp.int32),
            jax.ShapeDtypeStruct((1,), jnp.int32),
        ),
        in_specs=[
            pl.BlockSpec(memory_space=pltpu.SMEM),
            pl.BlockSpec(memory_space=pl.ANY),
            pl.BlockSpec(memory_space=pl.ANY),
        ],
        out_specs=tuple(whole(3)) + (pl.BlockSpec(memory_space=pltpu.SMEM),),
        scratch_shapes=[
            pltpu.VMEM((tokens, 16, width), BF16),
            pltpu.VMEM((1, width), F32),
            pltpu.VMEM((tokens, width), F32),
            pltpu.VMEM((tokens, 128), jnp.int32),
            pltpu.SMEM((tokens + 1,), jnp.int32),
            pltpu.SemaphoreType.DMA((tokens,)),
            pltpu.SemaphoreType.DMA,
        ],
        compiler_params=granted(48),
        name="lookup",
    )(token_ids.T, embed_table, norm_gain.reshape(1, width))

    arrived = lax.all_to_all(message, BOTH, 0, 0, tiled=True)

    def one_more(state):
        k, found = state
        rows = lax.dynamic_slice_in_dim(raw_rows, k * SLOTS, SLOTS, 0).astype(F32)
        meansq = jnp.mean(rows * rows, axis=-1, keepdims=True)
        rows = (rows * lax.rsqrt(meansq + EPS_NORM) * norm_gain).astype(BF16)
        rows = rows.reshape(SLOTS, dp * tp, depth).transpose(1, 0, 2)
        rows = lax.all_to_all(rows, BOTH, 0, 0, tiled=True).reshape(-1, depth)
        holder, rank = place[:, :1] // tokens, place[:, :1] % tokens
        at = jnp.where(rank // SLOTS == k, holder * SLOTS + rank % SLOTS, -1)
        select = (at == jnp.arange(dp * tp * SLOTS, dtype=jnp.int32)).astype(BF16)
        rows = jnp.dot(select, rows, preferred_element_type=F32).astype(BF16)
        return k + 1, found + jnp.pad(rows, ((0, 0), (0, 256 - depth)))

    def all_more(rounds):
        return lax.while_loop(
            lambda state: state[0] <= rounds,
            one_more,
            (jnp.int32(1), jnp.zeros((tokens, 256), BF16)),
        )[1]

    qkv_master_new, qkv_first_new, qkv_second_new = adamw(
        qkv_master, qkv_first, qkv_second, qkv_grad
    )
    out_master_new, out_first_new, out_second_new = adamw(
        out_master, out_first, out_second, out_grad
    )
    qkv_half = qkv_master_new.astype(BF16)
    out_half = out_master_new.astype(BF16)
    arrived, most = lax.optimization_barrier((arrived, most))
    extra = all_more(most[0] // SLOTS)

    keep, send = pl.pallas_call(
        functools.partial(project_kernel, dp, tp),
        out_shape=(jax.ShapeDtypeStruct((half, per_dp, joined_width), F32),) * 2,
        in_specs=whole(4),
        out_specs=tuple(whole(2)),
        compiler_params=granted(16),
        name="project",
    )(place, arrived, extra, qkv_half)
    partial = among_chips(keep + other_core(send))
    projected = jnp.sum(partial, axis=0).astype(BF16)
    joined = lax.all_to_all(
        jnp.broadcast_to(projected[None], (tp,) + projected.shape), "tp", 0, 0, tiled=True
    )

    messages = pl.pallas_call(
        functools.partial(attend_kernel, dp, tp),
        out_shape=jax.ShapeDtypeStruct((dp * tp, per_dp, 256), BF16),
        in_specs=[
            pl.BlockSpec(memory_space=pltpu.SMEM),
            pl.BlockSpec(memory_space=pltpu.VMEM),
            pl.BlockSpec(memory_space=pltpu.HBM),
            pl.BlockSpec(memory_space=pltpu.HBM),
        ],
        out_specs=pl.BlockSpec(memory_space=pltpu.VMEM),
        scratch_shapes=[
            pltpu.VMEM((group_rows, span, cache_keys.shape[2]), BF16),
            pltpu.VMEM((group_rows, span, cache_keys.shape[2]), BF16),
            pltpu.VMEM((KV_HEADS, GROUP * per_dp, span), F32),
            pltpu.VMEM((KV_HEADS, GROUP * per_dp, span), BF16),
            pltpu.VMEM((KV_HEADS, GROUP * per_dp, HEAD), F32),
            pltpu.VMEM((per_dp, width), F32),
            pltpu.SemaphoreType.DMA((group_rows,)),
            pltpu.SemaphoreType.DMA((group_rows,)),
        ],
        compiler_params=granted(56),
        name="attend",
    )(cache_lengths, joined, cache_keys, cache_values)
    arrived = lax.all_to_all(messages, BOTH, 0, 0, tiled=True)

    keep, send = pl.pallas_call(
        functools.partial(output_kernel, dp, tp),
        out_shape=(jax.ShapeDtypeStruct((half, per_dp, out_width), F32),) * 2,
        in_specs=whole(4),
        out_specs=tuple(whole(2)),
        compiler_params=granted(16),
        name="output",
    )(place, arrived, out_half, raw_rows)
    sums = among_chips((keep + other_core(send)).astype(BF16))
    layer_out = pl.pallas_call(
        finish_kernel,
        out_shape=jax.ShapeDtypeStruct((group_rows, STEPS, out_width), BF16),
        in_specs=whole(1),
        out_specs=whole(1)[0],
        compiler_params=granted(16),
        name="finish",
    )(sums)
    return (
        qkv_master_new,
        qkv_first_new,
        qkv_second_new,
        out_master_new,
        out_first_new,
        out_second_new,
        layer_out,
    )


def on_device_general(
    qkv_master,
    qkv_first,
    qkv_second,
    qkv_grad,
    out_master,
    out_first,
    out_second,
    out_grad,
    norm_gain,
    embed_table,
    cache_keys,
    cache_values,
    cache_lengths,
    token_ids,
):
    qkv_master_new, qkv_first_new, qkv_second_new = adamw(
        qkv_master, qkv_first, qkv_second, qkv_grad
    )
    out_master_new, out_first_new, out_second_new = adamw(
        out_master, out_first, out_second, out_grad
    )
    qkv_half = qkv_master_new.astype(jnp.bfloat16)
    out_half = out_master_new.astype(jnp.bfloat16)
    qkv_group, out_group = (
        lax.all_to_all(qkv_half, "tp", split_axis=1, concat_axis=0, tiled=True),
        lax.all_to_all(out_half, "tp", split_axis=1, concat_axis=0, tiled=True),
    )
    qkv_cols, out_cols = (
        lax.all_gather(qkv_group, "dp", axis=0, tiled=True),
        lax.all_gather(out_group, "dp", axis=0, tiled=True),
    )
    width = embed_table.shape[1]
    vocab_rows = embed_table.shape[0]
    group_rows = cache_keys.shape[0]
    first_entry = lax.axis_index(("dp", "tp")) * vocab_rows
    local_ids = token_ids.reshape(-1) - first_entry
    selector = (local_ids[:, None] == jnp.arange(vocab_rows, dtype=jnp.int32)[None, :]).astype(
        jnp.bfloat16
    )
    partial_rows = jnp.dot(selector, embed_table, preferred_element_type=jnp.float32).reshape(
        -1, 2, width
    )
    every_row = lax.psum(partial_rows, ("dp", "tp"))
    own_inputs = lax.dynamic_slice_in_dim(
        every_row, lax.axis_index("dp") * group_rows, group_rows, 0
    )
    meansq = jnp.mean(own_inputs * own_inputs, axis=-1, keepdims=True)
    normed = (own_inputs * lax.rsqrt(meansq + EPS_NORM) * norm_gain).astype(jnp.bfloat16)
    proj_part = jnp.dot(
        normed.reshape(-1, width), qkv_cols, preferred_element_type=jnp.float32
    ).astype(jnp.bfloat16)
    projected = lax.all_gather(proj_part, "tp", axis=1, tiled=True).reshape(group_rows, 2, -1)
    group_size = HEADS // KV_HEADS
    kv_width = KV_HEADS * HEAD
    scale_factor = HEAD ** (-0.5)
    queries = projected[..., :width].reshape(group_rows, 2, KV_HEADS, group_size, HEAD)
    fresh_keys = projected[..., width : width + kv_width].reshape(group_rows, 2, KV_HEADS, HEAD)
    fresh_values = projected[..., width + kv_width :].reshape(group_rows, 2, KV_HEADS, HEAD)
    span = cache_keys.shape[1]
    old_keys = cache_keys.reshape(group_rows, span, KV_HEADS, HEAD)
    old_values = cache_values.reshape(group_rows, span, KV_HEADS, HEAD)
    cache_scores = (
        jnp.einsum("rsghd,rpgd->rsghp", queries, old_keys, preferred_element_type=jnp.float32)
        * scale_factor
    )
    position = lax.axis_index("tp") * span + jnp.arange(span, dtype=jnp.int32)
    live = (position[None, :] < cache_lengths[:, None])[:, None, None, None, :]
    cache_scores = jnp.where(live, cache_scores, MASK_LOW)
    local_top = cache_scores.max(-1)
    cache_probs = jnp.where(live, jnp.exp(cache_scores - local_top[..., None]), 0.0)
    local_total = cache_probs.sum(-1)
    local_weighted = jnp.einsum(
        "rsghp,rpgd->rsghd", cache_probs, old_values, preferred_element_type=jnp.float32
    )
    cache_top = lax.pmax(local_top, "tp")
    rescale = jnp.exp(local_top - cache_top)
    cache_total, cache_weighted = lax.psum(
        (local_total * rescale, local_weighted * rescale[..., None]), "tp"
    )
    fresh_scores = (
        jnp.einsum("rsghd,rjgd->rsghj", queries, fresh_keys, preferred_element_type=jnp.float32)
        * scale_factor
    )
    causal = jnp.arange(2, dtype=jnp.int32)[None, :] <= jnp.arange(2, dtype=jnp.int32)[:, None]
    causal = causal[None, :, None, None, :]
    fresh_scores = jnp.where(causal, fresh_scores, MASK_LOW)
    highest = jnp.maximum(cache_top, fresh_scores.max(-1))
    cache_scale = jnp.exp(cache_top - highest)
    fresh_probs = jnp.where(causal, jnp.exp(fresh_scores - highest[..., None]), 0.0)
    totals = cache_total * cache_scale + fresh_probs.sum(-1)
    weighted = cache_weighted * cache_scale[..., None]
    weighted = weighted + jnp.einsum(
        "rsghj,rjgd->rsghd", fresh_probs, fresh_values.astype(jnp.float32)
    )
    attended = (weighted / totals[..., None]).reshape(group_rows * 2, width).astype(jnp.bfloat16)
    out_width = out_cols.shape[1]
    mixed = jnp.dot(attended, out_cols, preferred_element_type=jnp.float32).reshape(
        group_rows, 2, out_width
    )
    residual_cols = lax.dynamic_slice_in_dim(
        own_inputs, lax.axis_index("tp") * out_width, out_width, 2
    )
    layer_out = (residual_cols + mixed).astype(jnp.bfloat16)
    return (
        qkv_master_new,
        qkv_first_new,
        qkv_second_new,
        out_master_new,
        out_first_new,
        out_second_new,
        layer_out,
    )


def solution(mesh):
    dp, tp = mesh.shape["dp"], mesh.shape["tp"]
    placed = (
        P(("dp", "tp"), None),
        P(("dp", "tp"), None),
        P(("dp", "tp"), None),
        P(("dp", "tp"), None),
        P(("dp", "tp"), None),
        P(("dp", "tp"), None),
        P(("dp", "tp"), None),
        P(("dp", "tp"), None),
        P(),
        P(("dp", "tp"), None),
        P("dp", "tp", None),
        P("dp", "tp", None),
        P("dp"),
        P(),
    )
    body = on_device_general
    if (dp, tp) == (4, KV_HEADS):
        body = functools.partial(on_device_partial, dp, tp)
    return jax.shard_map(
        body,
        mesh=mesh,
        in_specs=placed,
        out_specs=(
            P(("dp", "tp"), None),
            P(("dp", "tp"), None),
            P(("dp", "tp"), None),
            P(("dp", "tp"), None),
            P(("dp", "tp"), None),
            P(("dp", "tp"), None),
            P("dp", None, "tp"),
        ),
        check_vma=False,
    )
```

```python
import functools

import jax
import jax.numpy as jnp
from jax import lax
from jax.experimental import pallas as pl
from jax.experimental.pallas import tpu as pltpu
from jax.sharding import PartitionSpec as P

HEADS = 40
KV_HEADS = 8
HEAD = 128
GROUP = HEADS // KV_HEADS
STEPS = 2
SLOTS = 8


BETA_ONE = 0.9
BETA_TWO = 0.95
LEARN_RATE = 0.004
WEIGHT_DECAY = 0.1
EPS_ADAM = 1e-08
EPS_NORM = 1e-06
CORR_ONE = 1.0 - 0.9**10
CORR_TWO = 1.0 - 0.95**10
MASK_LOW = -1e30
BOTH = ("dp", "tp")
F32 = jnp.float32
BF16 = jnp.bfloat16
MIB = 1024 * 1024


def adamw(master, first, second, grad):
    gradient = grad.astype(jnp.float32)
    first_new = BETA_ONE * first + (1.0 - BETA_ONE) * gradient
    second_new = BETA_TWO * second + (1.0 - BETA_TWO) * gradient * gradient
    update = first_new / CORR_ONE / (jnp.sqrt(second_new / CORR_TWO) + EPS_ADAM)
    master_new = master - LEARN_RATE * (update + WEIGHT_DECAY * master)
    return (master_new, first_new, second_new)


def lookup_kernel(dp, tp, ids_ref, table_ref, gain_ref, msg_ref, raw_ref, place_ref, most_ref,
                  buf, gain, raw, column, entries, sems, gain_sem):
    tokens, width = raw.shape
    per_dp = tokens // dp
    vocab_rows = table_ref.shape[0]
    whole = vocab_rows // 16 * 16
    left = vocab_rows - whole
    depth = width // (dp * tp)
    my_core = lax.axis_index("dp") % 2
    base = (lax.axis_index("dp") * tp + lax.axis_index("tp")) * vocab_rows
    gain_copy = pltpu.make_async_copy(gain_ref, gain, gain_sem)
    gain_copy.start()

    def whole_rows(entry, rank):
        start = pl.multiple_of(entry // 16 * 16, 16)
        return pltpu.make_async_copy(
            table_ref.at[pl.ds(start, 16)], buf.at[rank], sems.at[rank]
        )

    def last_rows(rank):
        return pltpu.make_async_copy(
            table_ref.at[pl.ds(whole, left)], buf.at[rank, pl.ds(0, left)], sems.at[rank]
        )

    def look(t, held):
        identity = ids_ref[t % STEPS, t // STEPS]
        group = t // per_dp
        line = (group % 2 ^ my_core) * (tokens // 2) + group // 2 * per_dp + t % per_dp
        column[pl.ds(line, 1), :] = jnp.full((1, 128), identity, jnp.int32)
        entry = identity - base
        entries[held] = entry
        mine = jnp.logical_and(entry >= 0, entry < vocab_rows)
        return held + mine.astype(jnp.int32)

    held = jnp.int32(0)
    for t in range(tokens):
        held = look(t, held)

    def fetch(rank, _):
        entry = entries[rank]

        @pl.when(entry < whole)
        def _():
            whole_rows(entry, rank).start()

        if left:
            @pl.when(entry >= whole)
            def _():
                last_rows(rank).start()

        return 0

    buf[0:SLOTS] = jnp.zeros((SLOTS, 16, width), BF16)
    lax.fori_loop(0, held, fetch, 0)
    raw_ref[SLOTS:] = jnp.zeros((tokens - SLOTS, width), BF16)
    line = lax.broadcasted_iota(jnp.int32, (tokens, 128), 0)
    inside = line % (tokens // 2)
    order = (inside // per_dp * 2 + (line // (tokens // 2) ^ my_core)) * per_dp + line % per_dp
    identity = column[...].astype(F32)
    holder = jnp.floor(identity * (1.0 / vocab_rows))
    holder = jnp.where(holder * vocab_rows > identity, holder - 1.0, holder)
    holder = jnp.where((holder + 1.0) * vocab_rows <= identity, holder + 1.0, holder)
    key = holder * tokens + order.astype(F32)
    turned = jnp.transpose(
        jnp.concatenate([key, jnp.full((128 - tokens, 128), -1.0, F32)], axis=0)
    )[0:1, :]
    before = (turned >= holder * tokens) & (turned < key)
    rank = jnp.sum(before.astype(F32), axis=1, keepdims=True)
    place_ref[...] = (holder * tokens + rank).astype(jnp.int32)
    most_ref[0] = jnp.max(rank).astype(jnp.int32)

    def arrive(rank):
        entry = entries[rank]

        @pl.when(entry < whole)
        def _():
            whole_rows(entry, rank).wait()

        if left:
            @pl.when(entry >= whole)
            def _():
                last_rows(rank).wait()

        return entry % 16

    source = jnp.full((SLOTS, 1), -1, jnp.int32)
    slot = lax.broadcasted_iota(jnp.int32, (SLOTS, 1), 0)
    for rank in range(SLOTS):
        @pl.when(rank < held)
        def _():
            arrive(rank)

        at = jnp.where(rank < held, rank * 16 + entries[rank] % 16, -1)
        source = jnp.where(slot == rank, at, source)
    select = (
        lax.broadcasted_iota(jnp.int32, (SLOTS, SLOTS * 16), 1) == source
    ).astype(BF16)
    rows = jnp.dot(
        select, buf[0:SLOTS].reshape(SLOTS * 16, width), preferred_element_type=F32
    )
    gain_copy.wait()
    scale = lax.rsqrt(jnp.mean(rows * rows, axis=-1, keepdims=True) + EPS_NORM)
    first = rows * scale * gain[...]
    for b in range(dp * tp):
        rest = jnp.concatenate(
            [
                first[:, depth * b + 128 : depth * (b + 1)],
                jnp.zeros((SLOTS, 256 - depth), F32),
            ],
            axis=1,
        )
        msg_ref[b] = jnp.concatenate(
            [first[:, depth * b : depth * b + 128], rest], axis=0
        ).astype(BF16)
    raw_ref[0:SLOTS] = rows.astype(BF16)

    @pl.when(held > SLOTS)
    def _():
        raw[...] = jnp.zeros_like(raw)
        raw[0:SLOTS] = rows

        def take(rank, _):
            picked = lax.broadcasted_iota(jnp.int32, (16, width), 0) == arrive(rank)
            raw[pl.ds(rank, 1), :] = jnp.sum(
                jnp.where(picked, buf[rank].astype(F32), 0.0), axis=0, keepdims=True
            )
            return 0

        lax.fori_loop(SLOTS, held, take, 0)
        raw_ref[...] = raw[...].astype(BF16)


def by_core(rows, dp, per_dp):
    even = lax.axis_index("dp") % 2 == 0
    mine, other = [], []
    for x in range(dp // 2):
        at_even = rows[(2 * x) * per_dp : (2 * x + 1) * per_dp]
        at_odd = rows[(2 * x + 1) * per_dp : (2 * x + 2) * per_dp]
        mine.append(jnp.where(even, at_even, at_odd))
        other.append(jnp.where(even, at_odd, at_even))
    return jnp.concatenate(mine + other, axis=0)


def project_kernel(dp, tp, place_ref, msg_ref, extra_ref, weight_ref, keep_ref, send_ref):
    tokens = place_ref.shape[0]
    per_dp = tokens // dp
    width = HEADS * HEAD
    kv_width = KV_HEADS * HEAD
    slots = dp * tp * SLOTS
    blocks = msg_ref[...].astype(F32)
    place = place_ref[:, 0:1]
    holder, rank = place // tokens, place % tokens
    place = jnp.where(rank < SLOTS, holder * SLOTS + rank, -1)
    select = (lax.broadcasted_iota(jnp.int32, (tokens, slots), 1) == place).astype(BF16)
    extra = extra_ref[...].astype(F32)

    def pick(rows, more):
        rows = rows.reshape(slots, 128).astype(BF16)
        return (jnp.dot(select, rows, preferred_element_type=F32) + more).astype(BF16)

    main = pick(blocks[:, :SLOTS], extra[:, :128])
    rest = pick(blocks[:, SLOTS:], extra[:, 128:])[:, : weight_ref.shape[0] - 128]
    half = tokens // 2

    def dot(at, size):
        return jnp.dot(
            main, weight_ref[0:128, at : at + size], preferred_element_type=F32
        ) + jnp.dot(rest, weight_ref[128:, at : at + size], preferred_element_type=F32)

    for g in range(tp):
        spans = (
            (0, g * GROUP * HEAD, GROUP * HEAD),
            (GROUP * HEAD, width + g * HEAD, HEAD),
            ((GROUP + 1) * HEAD, width + kv_width + g * HEAD, HEAD),
        )
        for to, at, size in spans:
            part = dot(at, size)
            for x in range(dp // 2):
                keep_ref[x * tp + g, :, to : to + size] = part[per_dp * x : per_dp * (x + 1)]
                send_ref[x * tp + g, :, to : to + size] = part[
                    half + per_dp * x : half + per_dp * (x + 1)
                ]


def attend_kernel(dp, tp, lengths_ref, qkv_ref, keys_ref, values_ref, msg_ref,
                  keys, values, scores_of, probs_of, weighted_of, joined, key_sems, value_sems):
    rows, span = keys.shape[0], keys.shape[1]
    per_dp = rows * STEPS
    lines = GROUP * per_dp
    my_tp = lax.axis_index("tp")
    depth = HEADS * HEAD // (dp * tp)
    scale = HEAD ** (-0.5)
    nt = (((1,), (1,)), ((), ()))

    def copies(source, target, sems):
        return [
            pltpu.make_async_copy(source.at[r], target.at[r], sems.at[r]) for r in range(rows)
        ]

    key_copies = copies(keys_ref, keys, key_sems)
    value_copies = copies(values_ref, values, value_sems)
    for copy in key_copies + value_copies:
        copy.start()

    line = lax.broadcasted_iota(jnp.int32, (lines, 1), 0) % per_dp
    row_of = line // STEPS
    length = jnp.zeros((lines, 1), jnp.int32)
    for r in range(rows):
        length = jnp.where(row_of == r, lengths_ref[r], length)
    position = my_tp * span + lax.broadcasted_iota(jnp.int32, (lines, span), 1)
    live = position < length
    column = lax.broadcasted_iota(jnp.int32, (lines, per_dp), 1)
    causal = (column // STEPS == row_of) & (column <= line)

    queries = []
    for g in range(KV_HEADS):
        queries.append(
            jnp.concatenate(
                [qkv_ref[g, :, HEAD * h : HEAD * (h + 1)] for h in range(GROUP)], axis=0
            )
        )
    for r in range(rows):
        key_copies[r].wait()
        for g in range(KV_HEADS):
            part = lax.dot_general(
                queries[g],
                keys[r, :, HEAD * g : HEAD * (g + 1)],
                nt,
                preferred_element_type=F32,
            )
            scores_of[g] = part if r == 0 else jnp.where(row_of == r, part, scores_of[g])
    kept = []
    for g in range(KV_HEADS):
        fresh_keys = qkv_ref[g, :, GROUP * HEAD : (GROUP + 1) * HEAD]
        fresh_values = qkv_ref[g, :, (GROUP + 1) * HEAD :]
        scores = jnp.where(live, scores_of[g] * scale, MASK_LOW)
        fresh = lax.dot_general(queries[g], fresh_keys, nt, preferred_element_type=F32) * scale
        seen = causal & (my_tp == g)
        fresh = jnp.where(seen, fresh, MASK_LOW)
        top = jnp.maximum(
            jnp.max(scores, axis=-1, keepdims=True), jnp.max(fresh, axis=-1, keepdims=True)
        )
        probs = jnp.where(live, jnp.exp(scores - top), 0.0)
        fresh_probs = jnp.where(seen, jnp.exp(fresh - top), 0.0)
        total = jnp.sum(probs, axis=-1, keepdims=True)
        total += jnp.sum(fresh_probs, axis=-1, keepdims=True)
        probs_of[g] = probs.astype(BF16)
        weighted_of[g] = jnp.dot(
            fresh_probs.astype(BF16), fresh_values, preferred_element_type=F32
        )
        kept.append((top, total))
    for r in range(rows):
        value_copies[r].wait()
        for g in range(KV_HEADS):
            probs = probs_of[g]
            weighted_of[g] += jnp.dot(
                jnp.where(row_of == r, probs, jnp.zeros_like(probs)),
                values[r, :, HEAD * g : HEAD * (g + 1)],
                preferred_element_type=F32,
            )

    lane = lax.broadcasted_iota(jnp.int32, (per_dp, HEAD), 1)
    levels = jnp.zeros((per_dp, HEAD), F32)
    for g in range(KV_HEADS):
        top, total = kept[g]
        some = total > 0.0
        safe = jnp.where(some, total, 1.0)
        outcome = weighted_of[g] / safe
        logsum = jnp.where(some, top + jnp.log(safe), MASK_LOW)
        for h in range(GROUP):
            head = g * GROUP + h
            joined[:, HEAD * head : HEAD * (head + 1)] = outcome[per_dp * h : per_dp * (h + 1)]
            one = logsum[per_dp * h : per_dp * (h + 1)]
            high = one.astype(BF16).astype(F32)
            middle = (one - high).astype(BF16).astype(F32)
            for i, part in enumerate((high, middle, one - high - middle)):
                levels = jnp.where(lane == 3 * head + i, part, levels)
    for b in range(dp * tp):
        at = depth * b
        turned = pltpu.roll(levels, (depth - 128 - 3 * (at // HEAD)) % 128, 1)
        rest = jnp.concatenate(
            [joined[:, at + 128 : at + depth], jnp.zeros((per_dp, 256 - depth), F32)], axis=1
        )
        rest = jnp.where(lane < depth - 128, rest, turned)
        msg_ref[b] = jnp.concatenate([joined[:, at : at + 128], rest], axis=1).astype(BF16)


def output_kernel(dp, tp, place_ref, msg_ref, weight_ref, raw_ref, keep_ref, send_ref):
    depth = weight_ref.shape[0]
    tokens, per_dp = place_ref.shape[0], msg_ref.shape[1]
    my_block = lax.axis_index("dp") * tp + lax.axis_index("tp")
    edge = HEAD - (depth * my_block) % HEAD
    first_head = lax.broadcasted_iota(jnp.int32, (per_dp, depth), 1) < edge
    merged = []
    for d in range(dp):
        parts, levels = [], []
        for t in range(tp):
            block = msg_ref[d * tp + t].astype(F32)
            stats = [block[:, depth + i : depth + i + 1] for i in range(6)]
            one = stats[0] + stats[1] + stats[2]
            two = stats[3] + stats[4] + stats[5]
            levels.append(jnp.where(first_head, one, two))
            parts.append(block[:, :depth])
        top = functools.reduce(jnp.maximum, levels)
        total = jnp.zeros_like(top)
        weighted = jnp.zeros_like(top)
        for part, lev in zip(parts, levels):
            share = jnp.exp(lev - top)
            total += share
            weighted += share * part
        merged.append(weighted / total)
    attended = by_core(jnp.concatenate(merged, axis=0), dp, per_dp).astype(BF16)
    place = place_ref[:, 0:1] - my_block * tokens
    select = (lax.broadcasted_iota(jnp.int32, (tokens, tokens), 1) == place).astype(BF16)
    half = tokens // 2
    out_width = weight_ref.shape[1] // tp
    for t in range(tp):
        cols = slice(out_width * t, out_width * (t + 1))
        part = jnp.dot(attended, weight_ref[:, cols], preferred_element_type=F32)
        part += jnp.dot(select, raw_ref[:, cols], preferred_element_type=F32)
        for x in range(dp // 2):
            keep_ref[x * tp + t] = part[per_dp * x : per_dp * (x + 1)]
            send_ref[x * tp + t] = part[half + per_dp * x : half + per_dp * (x + 1)]


def finish_kernel(sums_ref, out_ref):
    total = jnp.sum(sums_ref[...].astype(F32), axis=0)
    out_ref[...] = total.reshape(out_ref.shape).astype(BF16)


def whole(shape_count):
    return [pl.BlockSpec(memory_space=pltpu.VMEM)] * shape_count


def on_device_partial(
    dp,
    tp,
    qkv_master,
    qkv_first,
    qkv_second,
    qkv_grad,
    out_master,
    out_first,
    out_second,
    out_grad,
    norm_gain,
    embed_table,
    cache_keys,
    cache_values,
    cache_lengths,
    token_ids,
):
    width = embed_table.shape[1]
    group_rows, span = cache_keys.shape[0], cache_keys.shape[1]
    per_dp = group_rows * STEPS
    tokens = per_dp * dp
    half = dp // 2 * tp
    depth = width // (dp * tp)
    out_width = width // tp
    joined_width = (GROUP + 2) * HEAD

    def granted(size):
        return pltpu.CompilerParams(vmem_limit_bytes=size * MIB)


    core_pairs = [
        (d * tp + t, (d ^ 1) * tp + t) for d in range(dp) for t in range(tp)
    ]
    same_core = [
        [(2 * x + c) * tp + t for x in range(dp // 2) for t in range(tp)] for c in range(2)
    ]

    def other_core(value):
        return lax.ppermute(value, BOTH, core_pairs)

    def among_chips(value):
        return lax.all_to_all(value, BOTH, 0, 0, tiled=True, axis_index_groups=same_core)

    message, raw_rows, place, most = pl.pallas_call(
        functools.partial(lookup_kernel, dp, tp),
        out_shape=(
            jax.ShapeDtypeStruct((dp * tp, 2 * SLOTS, 128), BF16),
            jax.ShapeDtypeStruct((tokens, width), BF16),
            jax.ShapeDtypeStruct((tokens, 128), jnp.int32),
            jax.ShapeDtypeStruct((1,), jnp.int32),
        ),
        in_specs=[
            pl.BlockSpec(memory_space=pltpu.SMEM),
            pl.BlockSpec(memory_space=pl.ANY),
            pl.BlockSpec(memory_space=pl.ANY),
        ],
        out_specs=tuple(whole(3)) + (pl.BlockSpec(memory_space=pltpu.SMEM),),
        scratch_shapes=[
            pltpu.VMEM((tokens, 16, width), BF16),
            pltpu.VMEM((1, width), F32),
            pltpu.VMEM((tokens, width), F32),
            pltpu.VMEM((tokens, 128), jnp.int32),
            pltpu.SMEM((tokens + 1,), jnp.int32),
            pltpu.SemaphoreType.DMA((tokens,)),
            pltpu.SemaphoreType.DMA,
        ],
        compiler_params=granted(62),
        name="lookup",
    )(token_ids.T, embed_table, norm_gain.reshape(1, width))

    arrived = lax.all_to_all(message, BOTH, 0, 0, tiled=True)

    def one_more(state):
        k, found = state
        rows = lax.dynamic_slice_in_dim(raw_rows, k * SLOTS, SLOTS, 0).astype(F32)
        meansq = jnp.mean(rows * rows, axis=-1, keepdims=True)
        rows = (rows * lax.rsqrt(meansq + EPS_NORM) * norm_gain).astype(BF16)
        rows = rows.reshape(SLOTS, dp * tp, depth).transpose(1, 0, 2)
        rows = lax.all_to_all(rows, BOTH, 0, 0, tiled=True).reshape(-1, depth)
        holder, rank = place[:, :1] // tokens, place[:, :1] % tokens
        at = jnp.where(rank // SLOTS == k, holder * SLOTS + rank % SLOTS, -1)
        select = (at == jnp.arange(dp * tp * SLOTS, dtype=jnp.int32)).astype(BF16)
        rows = jnp.dot(select, rows, preferred_element_type=F32).astype(BF16)
        return k + 1, found + jnp.pad(rows, ((0, 0), (0, 256 - depth)))

    def all_more(rounds):
        return lax.while_loop(
            lambda state: state[0] <= rounds,
            one_more,
            (jnp.int32(1), jnp.zeros((tokens, 256), BF16)),
        )[1]

    qkv_master_new, qkv_first_new, qkv_second_new = adamw(
        qkv_master, qkv_first, qkv_second, qkv_grad
    )
    out_master_new, out_first_new, out_second_new = adamw(
        out_master, out_first, out_second, out_grad
    )
    qkv_half = qkv_master_new.astype(BF16)
    out_half = out_master_new.astype(BF16)
    arrived, most = lax.optimization_barrier((arrived, most))
    extra = all_more(most[0] // SLOTS)

    keep, send = pl.pallas_call(
        functools.partial(project_kernel, dp, tp),
        out_shape=(jax.ShapeDtypeStruct((half, per_dp, joined_width), F32),) * 2,
        in_specs=whole(4),
        out_specs=tuple(whole(2)),
        compiler_params=granted(16),
        name="project",
    )(place, arrived, extra, qkv_half)
    partial = among_chips(keep + other_core(send))
    projected = jnp.sum(partial, axis=0).astype(BF16)
    joined = lax.all_to_all(
        jnp.broadcast_to(projected[None], (tp,) + projected.shape), "tp", 0, 0, tiled=True
    )

    messages = pl.pallas_call(
        functools.partial(attend_kernel, dp, tp),
        out_shape=jax.ShapeDtypeStruct((dp * tp, per_dp, 256), BF16),
        in_specs=[
            pl.BlockSpec(memory_space=pltpu.SMEM),
            pl.BlockSpec(memory_space=pltpu.VMEM),
            pl.BlockSpec(memory_space=pltpu.HBM),
            pl.BlockSpec(memory_space=pltpu.HBM),
        ],
        out_specs=pl.BlockSpec(memory_space=pltpu.VMEM),
        scratch_shapes=[
            pltpu.VMEM((group_rows, span, cache_keys.shape[2]), BF16),
            pltpu.VMEM((group_rows, span, cache_keys.shape[2]), BF16),
            pltpu.VMEM((KV_HEADS, GROUP * per_dp, span), F32),
            pltpu.VMEM((KV_HEADS, GROUP * per_dp, span), BF16),
            pltpu.VMEM((KV_HEADS, GROUP * per_dp, HEAD), F32),
            pltpu.VMEM((per_dp, width), F32),
            pltpu.SemaphoreType.DMA((group_rows,)),
            pltpu.SemaphoreType.DMA((group_rows,)),
        ],
        compiler_params=granted(56),
        name="attend",
    )(cache_lengths, joined, cache_keys, cache_values)
    arrived = lax.all_to_all(messages, BOTH, 0, 0, tiled=True)

    keep, send = pl.pallas_call(
        functools.partial(output_kernel, dp, tp),
        out_shape=(jax.ShapeDtypeStruct((half, per_dp, out_width), F32),) * 2,
        in_specs=whole(4),
        out_specs=tuple(whole(2)),
        compiler_params=granted(16),
        name="output",
    )(place, arrived, out_half, raw_rows)
    sums = among_chips((keep + other_core(send)).astype(BF16))
    layer_out = pl.pallas_call(
        finish_kernel,
        out_shape=jax.ShapeDtypeStruct((group_rows, STEPS, out_width), BF16),
        in_specs=whole(1),
        out_specs=whole(1)[0],
        compiler_params=granted(16),
        name="finish",
    )(sums)
    return (
        qkv_master_new,
        qkv_first_new,
        qkv_second_new,
        out_master_new,
        out_first_new,
        out_second_new,
        layer_out,
    )


def on_device_general(
    qkv_master,
    qkv_first,
    qkv_second,
    qkv_grad,
    out_master,
    out_first,
    out_second,
    out_grad,
    norm_gain,
    embed_table,
    cache_keys,
    cache_values,
    cache_lengths,
    token_ids,
):
    qkv_master_new, qkv_first_new, qkv_second_new = adamw(
        qkv_master, qkv_first, qkv_second, qkv_grad
    )
    out_master_new, out_first_new, out_second_new = adamw(
        out_master, out_first, out_second, out_grad
    )
    qkv_half = qkv_master_new.astype(jnp.bfloat16)
    out_half = out_master_new.astype(jnp.bfloat16)
    qkv_group, out_group = (
        lax.all_to_all(qkv_half, "tp", split_axis=1, concat_axis=0, tiled=True),
        lax.all_to_all(out_half, "tp", split_axis=1, concat_axis=0, tiled=True),
    )
    qkv_cols, out_cols = (
        lax.all_gather(qkv_group, "dp", axis=0, tiled=True),
        lax.all_gather(out_group, "dp", axis=0, tiled=True),
    )
    width = embed_table.shape[1]
    vocab_rows = embed_table.shape[0]
    group_rows = cache_keys.shape[0]
    first_entry = lax.axis_index(("dp", "tp")) * vocab_rows
    local_ids = token_ids.reshape(-1) - first_entry
    selector = (local_ids[:, None] == jnp.arange(vocab_rows, dtype=jnp.int32)[None, :]).astype(
        jnp.bfloat16
    )
    partial_rows = jnp.dot(selector, embed_table, preferred_element_type=jnp.float32).reshape(
        -1, 2, width
    )
    every_row = lax.psum(partial_rows, ("dp", "tp"))
    own_inputs = lax.dynamic_slice_in_dim(
        every_row, lax.axis_index("dp") * group_rows, group_rows, 0
    )
    meansq = jnp.mean(own_inputs * own_inputs, axis=-1, keepdims=True)
    normed = (own_inputs * lax.rsqrt(meansq + EPS_NORM) * norm_gain).astype(jnp.bfloat16)
    proj_part = jnp.dot(
        normed.reshape(-1, width), qkv_cols, preferred_element_type=jnp.float32
    ).astype(jnp.bfloat16)
    projected = lax.all_gather(proj_part, "tp", axis=1, tiled=True).reshape(group_rows, 2, -1)
    group_size = HEADS // KV_HEADS
    kv_width = KV_HEADS * HEAD
    scale_factor = HEAD ** (-0.5)
    queries = projected[..., :width].reshape(group_rows, 2, KV_HEADS, group_size, HEAD)
    fresh_keys = projected[..., width : width + kv_width].reshape(group_rows, 2, KV_HEADS, HEAD)
    fresh_values = projected[..., width + kv_width :].reshape(group_rows, 2, KV_HEADS, HEAD)
    span = cache_keys.shape[1]
    old_keys = cache_keys.reshape(group_rows, span, KV_HEADS, HEAD)
    old_values = cache_values.reshape(group_rows, span, KV_HEADS, HEAD)
    cache_scores = (
        jnp.einsum("rsghd,rpgd->rsghp", queries, old_keys, preferred_element_type=jnp.float32)
        * scale_factor
    )
    position = lax.axis_index("tp") * span + jnp.arange(span, dtype=jnp.int32)
    live = (position[None, :] < cache_lengths[:, None])[:, None, None, None, :]
    cache_scores = jnp.where(live, cache_scores, MASK_LOW)
    local_top = cache_scores.max(-1)
    cache_probs = jnp.where(live, jnp.exp(cache_scores - local_top[..., None]), 0.0)
    local_total = cache_probs.sum(-1)
    local_weighted = jnp.einsum(
        "rsghp,rpgd->rsghd", cache_probs, old_values, preferred_element_type=jnp.float32
    )
    cache_top = lax.pmax(local_top, "tp")
    rescale = jnp.exp(local_top - cache_top)
    cache_total, cache_weighted = lax.psum(
        (local_total * rescale, local_weighted * rescale[..., None]), "tp"
    )
    fresh_scores = (
        jnp.einsum("rsghd,rjgd->rsghj", queries, fresh_keys, preferred_element_type=jnp.float32)
        * scale_factor
    )
    causal = jnp.arange(2, dtype=jnp.int32)[None, :] <= jnp.arange(2, dtype=jnp.int32)[:, None]
    causal = causal[None, :, None, None, :]
    fresh_scores = jnp.where(causal, fresh_scores, MASK_LOW)
    highest = jnp.maximum(cache_top, fresh_scores.max(-1))
    cache_scale = jnp.exp(cache_top - highest)
    fresh_probs = jnp.where(causal, jnp.exp(fresh_scores - highest[..., None]), 0.0)
    totals = cache_total * cache_scale + fresh_probs.sum(-1)
    weighted = cache_weighted * cache_scale[..., None]
    weighted = weighted + jnp.einsum(
        "rsghj,rjgd->rsghd", fresh_probs, fresh_values.astype(jnp.float32)
    )
    attended = (weighted / totals[..., None]).reshape(group_rows * 2, width).astype(jnp.bfloat16)
    out_width = out_cols.shape[1]
    mixed = jnp.dot(attended, out_cols, preferred_element_type=jnp.float32).reshape(
        group_rows, 2, out_width
    )
    residual_cols = lax.dynamic_slice_in_dim(
        own_inputs, lax.axis_index("tp") * out_width, out_width, 2
    )
    layer_out = (residual_cols + mixed).astype(jnp.bfloat16)
    return (
        qkv_master_new,
        qkv_first_new,
        qkv_second_new,
        out_master_new,
        out_first_new,
        out_second_new,
        layer_out,
    )


def solution(mesh):
    dp, tp = mesh.shape["dp"], mesh.shape["tp"]
    placed = (
        P(("dp", "tp"), None),
        P(("dp", "tp"), None),
        P(("dp", "tp"), None),
        P(("dp", "tp"), None),
        P(("dp", "tp"), None),
        P(("dp", "tp"), None),
        P(("dp", "tp"), None),
        P(("dp", "tp"), None),
        P(),
        P(("dp", "tp"), None),
        P("dp", "tp", None),
        P("dp", "tp", None),
        P("dp"),
        P(),
    )
    body = on_device_general
    if (dp, tp) == (4, KV_HEADS):
        body = functools.partial(on_device_partial, dp, tp)
    return jax.shard_map(
        body,
        mesh=mesh,
        in_specs=placed,
        out_specs=(
            P(("dp", "tp"), None),
            P(("dp", "tp"), None),
            P(("dp", "tp"), None),
            P(("dp", "tp"), None),
            P(("dp", "tp"), None),
            P(("dp", "tp"), None),
            P("dp", None, "tp"),
        ),
        check_vma=False,
    )
```

```python
import functools

import jax
import jax.numpy as jnp
from jax import lax
from jax.experimental import pallas as pl
from jax.experimental.pallas import tpu as pltpu
from jax.sharding import PartitionSpec as P

HEADS = 40
KV_HEADS = 8
HEAD = 128
GROUP = HEADS // KV_HEADS
STEPS = 2
SLOTS = 8


BETA_ONE = 0.9
BETA_TWO = 0.95
LEARN_RATE = 0.004
WEIGHT_DECAY = 0.1
EPS_ADAM = 1e-08
EPS_NORM = 1e-06
CORR_ONE = 1.0 - 0.9**10
CORR_TWO = 1.0 - 0.95**10
MASK_LOW = -1e30
BOTH = ("dp", "tp")
F32 = jnp.float32
BF16 = jnp.bfloat16
MIB = 1024 * 1024


def adamw(master, first, second, grad):
    gradient = grad.astype(jnp.float32)
    first_new = BETA_ONE * first + (1.0 - BETA_ONE) * gradient
    second_new = BETA_TWO * second + (1.0 - BETA_TWO) * gradient * gradient
    update = first_new / CORR_ONE / (jnp.sqrt(second_new / CORR_TWO) + EPS_ADAM)
    master_new = master - LEARN_RATE * (update + WEIGHT_DECAY * master)
    return (master_new, first_new, second_new)


def lookup_kernel(dp, tp, ids_ref, table_ref, gain_ref, msg_ref, raw_ref, place_ref, most_ref,
                  buf, gain, raw, column, entries, sems, gain_sem):
    tokens, width = raw.shape
    per_dp = tokens // dp
    vocab_rows = table_ref.shape[0]
    whole = vocab_rows // 16 * 16
    left = vocab_rows - whole
    depth = width // (dp * tp)
    my_core = lax.axis_index("dp") % 2
    base = (lax.axis_index("dp") * tp + lax.axis_index("tp")) * vocab_rows
    gain_copy = pltpu.make_async_copy(gain_ref, gain, gain_sem)
    gain_copy.start()

    def whole_rows(entry, rank):
        start = pl.multiple_of(entry // 16 * 16, 16)
        return pltpu.make_async_copy(
            table_ref.at[pl.ds(start, 16)], buf.at[rank], sems.at[rank]
        )

    def last_rows(rank):
        return pltpu.make_async_copy(
            table_ref.at[pl.ds(whole, left)], buf.at[rank, pl.ds(0, left)], sems.at[rank]
        )

    def look(t, held):
        identity = ids_ref[t % STEPS, t // STEPS]
        group = t // per_dp
        line = (group % 2 ^ my_core) * (tokens // 2) + group // 2 * per_dp + t % per_dp
        column[pl.ds(line, 1), :] = jnp.full((1, 128), identity, jnp.int32)
        entry = identity - base
        entries[held] = entry
        mine = jnp.logical_and(entry >= 0, entry < vocab_rows)
        return held + mine.astype(jnp.int32)

    held = jnp.int32(0)
    for t in range(tokens):
        held = look(t, held)

    def fetch(rank, _):
        entry = entries[rank]

        @pl.when(entry < whole)
        def _():
            whole_rows(entry, rank).start()

        if left:
            @pl.when(entry >= whole)
            def _():
                last_rows(rank).start()

        return 0

    buf[0:SLOTS] = jnp.zeros((SLOTS, 16, width), BF16)
    lax.fori_loop(0, held, fetch, 0)
    raw_ref[SLOTS:] = jnp.zeros((tokens - SLOTS, width), BF16)
    line = lax.broadcasted_iota(jnp.int32, (tokens, 128), 0)
    inside = line % (tokens // 2)
    order = (inside // per_dp * 2 + (line // (tokens // 2) ^ my_core)) * per_dp + line % per_dp
    identity = column[...].astype(F32)
    holder = jnp.floor(identity * (1.0 / vocab_rows))
    holder = jnp.where(holder * vocab_rows > identity, holder - 1.0, holder)
    holder = jnp.where((holder + 1.0) * vocab_rows <= identity, holder + 1.0, holder)
    key = holder * tokens + order.astype(F32)
    turned = jnp.transpose(
        jnp.concatenate([key, jnp.full((128 - tokens, 128), -1.0, F32)], axis=0)
    )[0:1, :]
    before = (turned >= holder * tokens) & (turned < key)
    rank = jnp.sum(before.astype(F32), axis=1, keepdims=True)
    place_ref[...] = (holder * tokens + rank).astype(jnp.int32)
    most_ref[0] = jnp.max(rank).astype(jnp.int32)

    def arrive(rank):
        entry = entries[rank]

        @pl.when(entry < whole)
        def _():
            whole_rows(entry, rank).wait()

        if left:
            @pl.when(entry >= whole)
            def _():
                last_rows(rank).wait()

        return entry % 16

    source = jnp.full((SLOTS, 1), -1, jnp.int32)
    slot = lax.broadcasted_iota(jnp.int32, (SLOTS, 1), 0)
    for rank in range(SLOTS):
        @pl.when(rank < held)
        def _():
            arrive(rank)

        at = jnp.where(rank < held, rank * 16 + entries[rank] % 16, -1)
        source = jnp.where(slot == rank, at, source)
    select = (
        lax.broadcasted_iota(jnp.int32, (SLOTS, SLOTS * 16), 1) == source
    ).astype(BF16)
    rows = jnp.dot(
        select, buf[0:SLOTS].reshape(SLOTS * 16, width), preferred_element_type=F32
    )
    gain_copy.wait()
    scale = lax.rsqrt(jnp.mean(rows * rows, axis=-1, keepdims=True) + EPS_NORM)
    first = rows * scale * gain[...]
    for b in range(dp * tp):
        rest = jnp.concatenate(
            [
                first[:, depth * b + 128 : depth * (b + 1)],
                jnp.zeros((SLOTS, 256 - depth), F32),
            ],
            axis=1,
        )
        msg_ref[b] = jnp.concatenate(
            [first[:, depth * b : depth * b + 128], rest], axis=0
        ).astype(BF16)
    raw_ref[0:SLOTS] = rows.astype(BF16)

    @pl.when(held > SLOTS)
    def _():
        raw[...] = jnp.zeros_like(raw)
        raw[0:SLOTS] = rows

        def take(rank, _):
            picked = lax.broadcasted_iota(jnp.int32, (16, width), 0) == arrive(rank)
            raw[pl.ds(rank, 1), :] = jnp.sum(
                jnp.where(picked, buf[rank].astype(F32), 0.0), axis=0, keepdims=True
            )
            return 0

        lax.fori_loop(SLOTS, held, take, 0)
        raw_ref[...] = raw[...].astype(BF16)


def by_core(rows, dp, per_dp):
    even = lax.axis_index("dp") % 2 == 0
    mine, other = [], []
    for x in range(dp // 2):
        at_even = rows[(2 * x) * per_dp : (2 * x + 1) * per_dp]
        at_odd = rows[(2 * x + 1) * per_dp : (2 * x + 2) * per_dp]
        mine.append(jnp.where(even, at_even, at_odd))
        other.append(jnp.where(even, at_odd, at_even))
    return jnp.concatenate(mine + other, axis=0)


def project_kernel(dp, tp, place_ref, msg_ref, extra_ref, weight_ref, keep_ref, send_ref):
    tokens = place_ref.shape[0]
    per_dp = tokens // dp
    width = HEADS * HEAD
    kv_width = KV_HEADS * HEAD
    slots = dp * tp * SLOTS
    blocks = msg_ref[...].astype(F32)
    place = place_ref[:, 0:1]
    holder, rank = place // tokens, place % tokens
    place = jnp.where(rank < SLOTS, holder * SLOTS + rank, -1)
    select = (lax.broadcasted_iota(jnp.int32, (tokens, slots), 1) == place).astype(BF16)
    extra = extra_ref[...].astype(F32)

    def pick(rows, more):
        rows = rows.reshape(slots, 128).astype(BF16)
        return (jnp.dot(select, rows, preferred_element_type=F32) + more).astype(BF16)

    main = pick(blocks[:, :SLOTS], extra[:, :128])
    rest = pick(blocks[:, SLOTS:], extra[:, 128:])[:, : weight_ref.shape[0] - 128]
    half = tokens // 2

    def dot(at, size):
        return jnp.dot(
            main, weight_ref[0:128, at : at + size], preferred_element_type=F32
        ) + jnp.dot(rest, weight_ref[128:, at : at + size], preferred_element_type=F32)

    my_x, my_tp = lax.axis_index("dp") // 2, lax.axis_index("tp")
    upper = per_dp // 2
    for g in range(tp):
        spans = (
            (0, g * GROUP * HEAD, GROUP * HEAD),
            (GROUP * HEAD, width + g * HEAD, HEAD),
            ((GROUP + 1) * HEAD, width + kv_width + g * HEAD, HEAD),
        )
        away = g ^ my_tp
        in_y, in_z = away % 2, away // 2
        for to, at, size in spans:
            part = dot(at, size)
            cols = slice(to, to + size)
            for x in range(dp // 2):
                in_x = x ^ my_x
                for ref, start in ((keep_ref, per_dp * x), (send_ref, half + per_dp * x)):
                    ref[0, in_x, in_y, in_z, :, cols] = part[start : start + upper]
                    ref[1, in_y, in_x, in_z, :, cols] = part[start + upper : start + per_dp]


def attend_kernel(dp, tp, lengths_ref, qkv_ref, keys_ref, values_ref, msg_ref,
                  keys, values, scores_of, probs_of, weighted_of, joined, key_sems, value_sems):
    rows, span = keys.shape[0], keys.shape[1]
    per_dp = rows * STEPS
    lines = GROUP * per_dp
    my_tp = lax.axis_index("tp")
    depth = HEADS * HEAD // (dp * tp)
    scale = HEAD ** (-0.5)
    nt = (((1,), (1,)), ((), ()))

    def copies(source, target, sems):
        return [
            pltpu.make_async_copy(source.at[r], target.at[r], sems.at[r]) for r in range(rows)
        ]

    key_copies = copies(keys_ref, keys, key_sems)
    value_copies = copies(values_ref, values, value_sems)
    for copy in key_copies + value_copies:
        copy.start()

    line = lax.broadcasted_iota(jnp.int32, (lines, 1), 0) % per_dp
    row_of = line // STEPS
    length = jnp.zeros((lines, 1), jnp.int32)
    for r in range(rows):
        length = jnp.where(row_of == r, lengths_ref[r], length)
    position = my_tp * span + lax.broadcasted_iota(jnp.int32, (lines, span), 1)
    live = position < length
    column = lax.broadcasted_iota(jnp.int32, (lines, per_dp), 1)
    causal = (column // STEPS == row_of) & (column <= line)

    queries = []
    for g in range(KV_HEADS):
        queries.append(
            jnp.concatenate(
                [qkv_ref[g, :, HEAD * h : HEAD * (h + 1)] for h in range(GROUP)], axis=0
            )
        )
    for r in range(rows):
        key_copies[r].wait()
        for g in range(KV_HEADS):
            part = lax.dot_general(
                queries[g],
                keys[r, :, HEAD * g : HEAD * (g + 1)],
                nt,
                preferred_element_type=F32,
            )
            scores_of[g] = part if r == 0 else jnp.where(row_of == r, part, scores_of[g])
    kept = []
    for g in range(KV_HEADS):
        fresh_keys = qkv_ref[g, :, GROUP * HEAD : (GROUP + 1) * HEAD]
        fresh_values = qkv_ref[g, :, (GROUP + 1) * HEAD :]
        scores = jnp.where(live, scores_of[g] * scale, MASK_LOW)
        fresh = lax.dot_general(queries[g], fresh_keys, nt, preferred_element_type=F32) * scale
        seen = causal & (my_tp == g)
        fresh = jnp.where(seen, fresh, MASK_LOW)
        top = jnp.maximum(
            jnp.max(scores, axis=-1, keepdims=True), jnp.max(fresh, axis=-1, keepdims=True)
        )
        probs = jnp.where(live, jnp.exp(scores - top), 0.0)
        fresh_probs = jnp.where(seen, jnp.exp(fresh - top), 0.0)
        total = jnp.sum(probs, axis=-1, keepdims=True)
        total += jnp.sum(fresh_probs, axis=-1, keepdims=True)
        probs_of[g] = probs.astype(BF16)
        weighted_of[g] = jnp.dot(
            fresh_probs.astype(BF16), fresh_values, preferred_element_type=F32
        )
        kept.append((top, total))
    for r in range(rows):
        value_copies[r].wait()
        for g in range(KV_HEADS):
            probs = probs_of[g]
            weighted_of[g] += jnp.dot(
                jnp.where(row_of == r, probs, jnp.zeros_like(probs)),
                values[r, :, HEAD * g : HEAD * (g + 1)],
                preferred_element_type=F32,
            )

    lane = lax.broadcasted_iota(jnp.int32, (per_dp, HEAD), 1)
    levels = jnp.zeros((per_dp, HEAD), F32)
    for g in range(KV_HEADS):
        top, total = kept[g]
        some = total > 0.0
        safe = jnp.where(some, total, 1.0)
        outcome = weighted_of[g] / safe
        logsum = jnp.where(some, top + jnp.log(safe), MASK_LOW)
        for h in range(GROUP):
            head = g * GROUP + h
            joined[:, HEAD * head : HEAD * (head + 1)] = outcome[per_dp * h : per_dp * (h + 1)]
            one = logsum[per_dp * h : per_dp * (h + 1)]
            high = one.astype(BF16).astype(F32)
            middle = (one - high).astype(BF16).astype(F32)
            for i, part in enumerate((high, middle, one - high - middle)):
                levels = jnp.where(lane == 3 * head + i, part, levels)
    for b in range(dp * tp):
        at = depth * b
        turned = pltpu.roll(levels, (depth - 128 - 3 * (at // HEAD)) % 128, 1)
        rest = jnp.concatenate(
            [joined[:, at + 128 : at + depth], jnp.zeros((per_dp, 256 - depth), F32)], axis=1
        )
        rest = jnp.where(lane < depth - 128, rest, turned)
        msg_ref[b] = jnp.concatenate([joined[:, at : at + 128], rest], axis=1).astype(BF16)


def output_kernel(dp, tp, place_ref, msg_ref, weight_ref, raw_ref, keep_ref, send_ref):
    depth = weight_ref.shape[0]
    tokens, per_dp = place_ref.shape[0], msg_ref.shape[1]
    my_block = lax.axis_index("dp") * tp + lax.axis_index("tp")
    edge = HEAD - (depth * my_block) % HEAD
    first_head = lax.broadcasted_iota(jnp.int32, (per_dp, depth), 1) < edge
    merged = []
    for d in range(dp):
        parts, levels = [], []
        for t in range(tp):
            block = msg_ref[d * tp + t].astype(F32)
            stats = [block[:, depth + i : depth + i + 1] for i in range(6)]
            one = stats[0] + stats[1] + stats[2]
            two = stats[3] + stats[4] + stats[5]
            levels.append(jnp.where(first_head, one, two))
            parts.append(block[:, :depth])
        top = functools.reduce(jnp.maximum, levels)
        total = jnp.zeros_like(top)
        weighted = jnp.zeros_like(top)
        for part, lev in zip(parts, levels):
            share = jnp.exp(lev - top)
            total += share
            weighted += share * part
        merged.append(weighted / total)
    attended = by_core(jnp.concatenate(merged, axis=0), dp, per_dp).astype(BF16)
    place = place_ref[:, 0:1] - my_block * tokens
    select = (lax.broadcasted_iota(jnp.int32, (tokens, tokens), 1) == place).astype(BF16)
    half = tokens // 2
    out_width = weight_ref.shape[1] // tp
    for t in range(tp):
        cols = slice(out_width * t, out_width * (t + 1))
        part = jnp.dot(attended, weight_ref[:, cols], preferred_element_type=F32)
        part += jnp.dot(select, raw_ref[:, cols], preferred_element_type=F32)
        for x in range(dp // 2):
            keep_ref[x * tp + t] = part[per_dp * x : per_dp * (x + 1)]
            send_ref[x * tp + t] = part[half + per_dp * x : half + per_dp * (x + 1)]


def finish_kernel(sums_ref, out_ref):
    total = jnp.sum(sums_ref[...].astype(F32), axis=0)
    out_ref[...] = total.reshape(out_ref.shape).astype(BF16)


def whole(shape_count):
    return [pl.BlockSpec(memory_space=pltpu.VMEM)] * shape_count


def on_device_partial(
    dp,
    tp,
    qkv_master,
    qkv_first,
    qkv_second,
    qkv_grad,
    out_master,
    out_first,
    out_second,
    out_grad,
    norm_gain,
    embed_table,
    cache_keys,
    cache_values,
    cache_lengths,
    token_ids,
):
    width = embed_table.shape[1]
    group_rows, span = cache_keys.shape[0], cache_keys.shape[1]
    per_dp = group_rows * STEPS
    tokens = per_dp * dp
    half = dp // 2 * tp
    depth = width // (dp * tp)
    out_width = width // tp
    joined_width = (GROUP + 2) * HEAD

    def granted(size):
        return pltpu.CompilerParams(vmem_limit_bytes=size * MIB)


    core_pairs = [
        (d * tp + t, (d ^ 1) * tp + t) for d in range(dp) for t in range(tp)
    ]
    same_core = [
        [(2 * x + c) * tp + t for x in range(dp // 2) for t in range(tp)] for c in range(2)
    ]

    def other_core(value):
        return lax.ppermute(value, BOTH, core_pairs)

    def neighbour(value, flip):
        pairs = [
            (d * tp + t, (d ^ flip[0]) * tp + (t ^ flip[1])) for d in range(dp) for t in range(tp)
        ]
        return lax.ppermute(value, BOTH, pairs)

    def among_chips(value):
        return lax.all_to_all(value, BOTH, 0, 0, tiled=True, axis_index_groups=same_core)

    message, raw_rows, place, most = pl.pallas_call(
        functools.partial(lookup_kernel, dp, tp),
        out_shape=(
            jax.ShapeDtypeStruct((dp * tp, 2 * SLOTS, 128), BF16),
            jax.ShapeDtypeStruct((tokens, width), BF16),
            jax.ShapeDtypeStruct((tokens, 128), jnp.int32),
            jax.ShapeDtypeStruct((1,), jnp.int32),
        ),
        in_specs=[
            pl.BlockSpec(memory_space=pltpu.SMEM),
            pl.BlockSpec(memory_space=pl.ANY),
            pl.BlockSpec(memory_space=pl.ANY),
        ],
        out_specs=tuple(whole(3)) + (pl.BlockSpec(memory_space=pltpu.SMEM),),
        scratch_shapes=[
            pltpu.VMEM((tokens, 16, width), BF16),
            pltpu.VMEM((1, width), F32),
            pltpu.VMEM((tokens, width), F32),
            pltpu.VMEM((tokens, 128), jnp.int32),
            pltpu.SMEM((tokens + 1,), jnp.int32),
            pltpu.SemaphoreType.DMA((tokens,)),
            pltpu.SemaphoreType.DMA,
        ],
        compiler_params=granted(62),
        name="lookup",
    )(token_ids.T, embed_table, norm_gain.reshape(1, width))

    arrived = lax.all_to_all(message, BOTH, 0, 0, tiled=True)

    def one_more(state):
        k, found = state
        rows = lax.dynamic_slice_in_dim(raw_rows, k * SLOTS, SLOTS, 0).astype(F32)
        meansq = jnp.mean(rows * rows, axis=-1, keepdims=True)
        rows = (rows * lax.rsqrt(meansq + EPS_NORM) * norm_gain).astype(BF16)
        rows = rows.reshape(SLOTS, dp * tp, depth).transpose(1, 0, 2)
        rows = lax.all_to_all(rows, BOTH, 0, 0, tiled=True).reshape(-1, depth)
        holder, rank = place[:, :1] // tokens, place[:, :1] % tokens
        at = jnp.where(rank // SLOTS == k, holder * SLOTS + rank % SLOTS, -1)
        select = (at == jnp.arange(dp * tp * SLOTS, dtype=jnp.int32)).astype(BF16)
        rows = jnp.dot(select, rows, preferred_element_type=F32).astype(BF16)
        return k + 1, found + jnp.pad(rows, ((0, 0), (0, 256 - depth)))

    def all_more(rounds):
        return lax.while_loop(
            lambda state: state[0] <= rounds,
            one_more,
            (jnp.int32(1), jnp.zeros((tokens, 256), BF16)),
        )[1]

    qkv_master_new, qkv_first_new, qkv_second_new = adamw(
        qkv_master, qkv_first, qkv_second, qkv_grad
    )
    out_master_new, out_first_new, out_second_new = adamw(
        out_master, out_first, out_second, out_grad
    )
    qkv_half = qkv_master_new.astype(BF16)
    out_half = out_master_new.astype(BF16)
    arrived, most = lax.optimization_barrier((arrived, most))
    extra = all_more(most[0] // SLOTS)

    keep, send = pl.pallas_call(
        functools.partial(project_kernel, dp, tp),
        out_shape=(
            jax.ShapeDtypeStruct((2, 2, 2, tp // 2, per_dp // 2, joined_width), F32),
        ) * 2,
        in_specs=whole(4),
        out_specs=tuple(whole(2)),
        compiler_params=granted(16),
        name="project",
    )(place, arrived, extra, qkv_half)
    arrived = other_core(send)

    def fold(across, where):
        pairs = [(mine[0], neighbour(mine[1], flip)) for mine, flip in zip(across, where)]
        return [near + came for near, came in pairs]

    halves = [
        [keep[i, j] + arrived[i, j] for j in range(2)] for i in range(2)
    ]
    halves = fold(halves, ((2, 0), (0, 1)))
    halves = fold(halves, ((0, 1), (2, 0)))
    total = jnp.concatenate(halves, axis=1)
    flip = tp // 2
    while total.shape[0] > 1:
        count = total.shape[0] // 2
        total = total[:count] + neighbour(total[count:], (0, flip))
        flip //= 2
    projected = total[0].astype(BF16)
    joined = lax.all_to_all(
        jnp.broadcast_to(projected[None], (tp,) + projected.shape), "tp", 0, 0, tiled=True
    )

    messages = pl.pallas_call(
        functools.partial(attend_kernel, dp, tp),
        out_shape=jax.ShapeDtypeStruct((dp * tp, per_dp, 256), BF16),
        in_specs=[
            pl.BlockSpec(memory_space=pltpu.SMEM),
            pl.BlockSpec(memory_space=pltpu.VMEM),
            pl.BlockSpec(memory_space=pltpu.HBM),
            pl.BlockSpec(memory_space=pltpu.HBM),
        ],
        out_specs=pl.BlockSpec(memory_space=pltpu.VMEM),
        scratch_shapes=[
            pltpu.VMEM((group_rows, span, cache_keys.shape[2]), BF16),
            pltpu.VMEM((group_rows, span, cache_keys.shape[2]), BF16),
            pltpu.VMEM((KV_HEADS, GROUP * per_dp, span), F32),
            pltpu.VMEM((KV_HEADS, GROUP * per_dp, span), BF16),
            pltpu.VMEM((KV_HEADS, GROUP * per_dp, HEAD), F32),
            pltpu.VMEM((per_dp, width), F32),
            pltpu.SemaphoreType.DMA((group_rows,)),
            pltpu.SemaphoreType.DMA((group_rows,)),
        ],
        compiler_params=granted(56),
        name="attend",
    )(cache_lengths, joined, cache_keys, cache_values)
    arrived = lax.all_to_all(messages, BOTH, 0, 0, tiled=True)

    keep, send = pl.pallas_call(
        functools.partial(output_kernel, dp, tp),
        out_shape=(jax.ShapeDtypeStruct((half, per_dp, out_width), F32),) * 2,
        in_specs=whole(4),
        out_specs=tuple(whole(2)),
        compiler_params=granted(16),
        name="output",
    )(place, arrived, out_half, raw_rows)
    sums = among_chips((keep + other_core(send)).astype(BF16))
    layer_out = pl.pallas_call(
        finish_kernel,
        out_shape=jax.ShapeDtypeStruct((group_rows, STEPS, out_width), BF16),
        in_specs=whole(1),
        out_specs=whole(1)[0],
        compiler_params=granted(16),
        name="finish",
    )(sums)
    return (
        qkv_master_new,
        qkv_first_new,
        qkv_second_new,
        out_master_new,
        out_first_new,
        out_second_new,
        layer_out,
    )


def on_device_general(
    qkv_master,
    qkv_first,
    qkv_second,
    qkv_grad,
    out_master,
    out_first,
    out_second,
    out_grad,
    norm_gain,
    embed_table,
    cache_keys,
    cache_values,
    cache_lengths,
    token_ids,
):
    qkv_master_new, qkv_first_new, qkv_second_new = adamw(
        qkv_master, qkv_first, qkv_second, qkv_grad
    )
    out_master_new, out_first_new, out_second_new = adamw(
        out_master, out_first, out_second, out_grad
    )
    qkv_half = qkv_master_new.astype(jnp.bfloat16)
    out_half = out_master_new.astype(jnp.bfloat16)
    qkv_group, out_group = (
        lax.all_to_all(qkv_half, "tp", split_axis=1, concat_axis=0, tiled=True),
        lax.all_to_all(out_half, "tp", split_axis=1, concat_axis=0, tiled=True),
    )
    qkv_cols, out_cols = (
        lax.all_gather(qkv_group, "dp", axis=0, tiled=True),
        lax.all_gather(out_group, "dp", axis=0, tiled=True),
    )
    width = embed_table.shape[1]
    vocab_rows = embed_table.shape[0]
    group_rows = cache_keys.shape[0]
    first_entry = lax.axis_index(("dp", "tp")) * vocab_rows
    local_ids = token_ids.reshape(-1) - first_entry
    selector = (local_ids[:, None] == jnp.arange(vocab_rows, dtype=jnp.int32)[None, :]).astype(
        jnp.bfloat16
    )
    partial_rows = jnp.dot(selector, embed_table, preferred_element_type=jnp.float32).reshape(
        -1, 2, width
    )
    every_row = lax.psum(partial_rows, ("dp", "tp"))
    own_inputs = lax.dynamic_slice_in_dim(
        every_row, lax.axis_index("dp") * group_rows, group_rows, 0
    )
    meansq = jnp.mean(own_inputs * own_inputs, axis=-1, keepdims=True)
    normed = (own_inputs * lax.rsqrt(meansq + EPS_NORM) * norm_gain).astype(jnp.bfloat16)
    proj_part = jnp.dot(
        normed.reshape(-1, width), qkv_cols, preferred_element_type=jnp.float32
    ).astype(jnp.bfloat16)
    projected = lax.all_gather(proj_part, "tp", axis=1, tiled=True).reshape(group_rows, 2, -1)
    group_size = HEADS // KV_HEADS
    kv_width = KV_HEADS * HEAD
    scale_factor = HEAD ** (-0.5)
    queries = projected[..., :width].reshape(group_rows, 2, KV_HEADS, group_size, HEAD)
    fresh_keys = projected[..., width : width + kv_width].reshape(group_rows, 2, KV_HEADS, HEAD)
    fresh_values = projected[..., width + kv_width :].reshape(group_rows, 2, KV_HEADS, HEAD)
    span = cache_keys.shape[1]
    old_keys = cache_keys.reshape(group_rows, span, KV_HEADS, HEAD)
    old_values = cache_values.reshape(group_rows, span, KV_HEADS, HEAD)
    cache_scores = (
        jnp.einsum("rsghd,rpgd->rsghp", queries, old_keys, preferred_element_type=jnp.float32)
        * scale_factor
    )
    position = lax.axis_index("tp") * span + jnp.arange(span, dtype=jnp.int32)
    live = (position[None, :] < cache_lengths[:, None])[:, None, None, None, :]
    cache_scores = jnp.where(live, cache_scores, MASK_LOW)
    local_top = cache_scores.max(-1)
    cache_probs = jnp.where(live, jnp.exp(cache_scores - local_top[..., None]), 0.0)
    local_total = cache_probs.sum(-1)
    local_weighted = jnp.einsum(
        "rsghp,rpgd->rsghd", cache_probs, old_values, preferred_element_type=jnp.float32
    )
    cache_top = lax.pmax(local_top, "tp")
    rescale = jnp.exp(local_top - cache_top)
    cache_total, cache_weighted = lax.psum(
        (local_total * rescale, local_weighted * rescale[..., None]), "tp"
    )
    fresh_scores = (
        jnp.einsum("rsghd,rjgd->rsghj", queries, fresh_keys, preferred_element_type=jnp.float32)
        * scale_factor
    )
    causal = jnp.arange(2, dtype=jnp.int32)[None, :] <= jnp.arange(2, dtype=jnp.int32)[:, None]
    causal = causal[None, :, None, None, :]
    fresh_scores = jnp.where(causal, fresh_scores, MASK_LOW)
    highest = jnp.maximum(cache_top, fresh_scores.max(-1))
    cache_scale = jnp.exp(cache_top - highest)
    fresh_probs = jnp.where(causal, jnp.exp(fresh_scores - highest[..., None]), 0.0)
    totals = cache_total * cache_scale + fresh_probs.sum(-1)
    weighted = cache_weighted * cache_scale[..., None]
    weighted = weighted + jnp.einsum(
        "rsghj,rjgd->rsghd", fresh_probs, fresh_values.astype(jnp.float32)
    )
    attended = (weighted / totals[..., None]).reshape(group_rows * 2, width).astype(jnp.bfloat16)
    out_width = out_cols.shape[1]
    mixed = jnp.dot(attended, out_cols, preferred_element_type=jnp.float32).reshape(
        group_rows, 2, out_width
    )
    residual_cols = lax.dynamic_slice_in_dim(
        own_inputs, lax.axis_index("tp") * out_width, out_width, 2
    )
    layer_out = (residual_cols + mixed).astype(jnp.bfloat16)
    return (
        qkv_master_new,
        qkv_first_new,
        qkv_second_new,
        out_master_new,
        out_first_new,
        out_second_new,
        layer_out,
    )


def solution(mesh):
    dp, tp = mesh.shape["dp"], mesh.shape["tp"]
    placed = (
        P(("dp", "tp"), None),
        P(("dp", "tp"), None),
        P(("dp", "tp"), None),
        P(("dp", "tp"), None),
        P(("dp", "tp"), None),
        P(("dp", "tp"), None),
        P(("dp", "tp"), None),
        P(("dp", "tp"), None),
        P(),
        P(("dp", "tp"), None),
        P("dp", "tp", None),
        P("dp", "tp", None),
        P("dp"),
        P(),
    )
    body = on_device_general
    if (dp, tp) == (4, KV_HEADS):
        body = functools.partial(on_device_partial, dp, tp)
    return jax.shard_map(
        body,
        mesh=mesh,
        in_specs=placed,
        out_specs=(
            P(("dp", "tp"), None),
            P(("dp", "tp"), None),
            P(("dp", "tp"), None),
            P(("dp", "tp"), None),
            P(("dp", "tp"), None),
            P(("dp", "tp"), None),
            P("dp", None, "tp"),
        ),
        check_vma=False,
    )
```

```python
import functools

import jax
import jax.numpy as jnp
from jax import lax
from jax.experimental import pallas as pl
from jax.experimental.pallas import tpu as pltpu
from jax.sharding import PartitionSpec as P

HEADS = 40
KV_HEADS = 8
HEAD = 128
GROUP = HEADS // KV_HEADS
STEPS = 2
SLOTS = 8


BETA_ONE = 0.9
BETA_TWO = 0.95
LEARN_RATE = 0.004
WEIGHT_DECAY = 0.1
EPS_ADAM = 1e-08
EPS_NORM = 1e-06
CORR_ONE = 1.0 - 0.9**10
CORR_TWO = 1.0 - 0.95**10
MASK_LOW = -1e30
BOTH = ("dp", "tp")
F32 = jnp.float32
BF16 = jnp.bfloat16
MIB = 1024 * 1024


def adamw(master, first, second, grad):
    gradient = grad.astype(jnp.float32)
    first_new = BETA_ONE * first + (1.0 - BETA_ONE) * gradient
    second_new = BETA_TWO * second + (1.0 - BETA_TWO) * gradient * gradient
    update = first_new / CORR_ONE / (jnp.sqrt(second_new / CORR_TWO) + EPS_ADAM)
    master_new = master - LEARN_RATE * (update + WEIGHT_DECAY * master)
    return (master_new, first_new, second_new)


def lookup_kernel(dp, tp, ids_ref, table_ref, gain_ref, msg_ref, raw_ref, place_ref, most_ref,
                  buf, gain, raw, column, entries, sems, gain_sem):
    tokens, width = raw.shape
    per_dp = tokens // dp
    vocab_rows = table_ref.shape[0]
    whole = vocab_rows // 16 * 16
    left = vocab_rows - whole
    depth = width // (dp * tp)
    my_core = lax.axis_index("dp") % 2
    base = (lax.axis_index("dp") * tp + lax.axis_index("tp")) * vocab_rows
    gain_copy = pltpu.make_async_copy(gain_ref, gain, gain_sem)
    gain_copy.start()

    def whole_rows(entry, rank):
        start = pl.multiple_of(entry // 16 * 16, 16)
        return pltpu.make_async_copy(
            table_ref.at[pl.ds(start, 16)], buf.at[rank], sems.at[rank]
        )

    def last_rows(rank):
        return pltpu.make_async_copy(
            table_ref.at[pl.ds(whole, left)], buf.at[rank, pl.ds(0, left)], sems.at[rank]
        )

    def look(t, held):
        identity = ids_ref[t % STEPS, t // STEPS]
        group = t // per_dp
        line = (group % 2 ^ my_core) * (tokens // 2) + group // 2 * per_dp + t % per_dp
        column[pl.ds(line, 1), :] = jnp.full((1, 128), identity, jnp.int32)
        entry = identity - base
        entries[held] = entry
        mine = jnp.logical_and(entry >= 0, entry < vocab_rows)
        return held + mine.astype(jnp.int32)

    held = jnp.int32(0)
    for t in range(tokens):
        held = look(t, held)

    def fetch(rank, _):
        entry = entries[rank]

        @pl.when(entry < whole)
        def _():
            whole_rows(entry, rank).start()

        if left:
            @pl.when(entry >= whole)
            def _():
                last_rows(rank).start()

        return 0

    buf[0:SLOTS] = jnp.zeros((SLOTS, 16, width), BF16)
    lax.fori_loop(0, held, fetch, 0)
    raw_ref[SLOTS:] = jnp.zeros((tokens - SLOTS, width), BF16)
    line = lax.broadcasted_iota(jnp.int32, (tokens, 128), 0)
    inside = line % (tokens // 2)
    order = (inside // per_dp * 2 + (line // (tokens // 2) ^ my_core)) * per_dp + line % per_dp
    identity = column[...].astype(F32)
    holder = jnp.floor(identity * (1.0 / vocab_rows))
    holder = jnp.where(holder * vocab_rows > identity, holder - 1.0, holder)
    holder = jnp.where((holder + 1.0) * vocab_rows <= identity, holder + 1.0, holder)
    key = holder * tokens + order.astype(F32)
    turned = jnp.transpose(
        jnp.concatenate([key, jnp.full((128 - tokens, 128), -1.0, F32)], axis=0)
    )[0:1, :]
    before = (turned >= holder * tokens) & (turned < key)
    rank = jnp.sum(before.astype(F32), axis=1, keepdims=True)
    place_ref[...] = (holder * tokens + rank).astype(jnp.int32)
    most_ref[0] = jnp.max(rank).astype(jnp.int32)

    def arrive(rank):
        entry = entries[rank]

        @pl.when(entry < whole)
        def _():
            whole_rows(entry, rank).wait()

        if left:
            @pl.when(entry >= whole)
            def _():
                last_rows(rank).wait()

        return entry % 16

    source = jnp.full((SLOTS, 1), -1, jnp.int32)
    slot = lax.broadcasted_iota(jnp.int32, (SLOTS, 1), 0)
    for rank in range(SLOTS):
        @pl.when(rank < held)
        def _():
            arrive(rank)

        at = jnp.where(rank < held, rank * 16 + entries[rank] % 16, -1)
        source = jnp.where(slot == rank, at, source)
    select = (
        lax.broadcasted_iota(jnp.int32, (SLOTS, SLOTS * 16), 1) == source
    ).astype(BF16)
    rows = jnp.dot(
        select, buf[0:SLOTS].reshape(SLOTS * 16, width), preferred_element_type=F32
    )
    gain_copy.wait()
    scale = lax.rsqrt(jnp.mean(rows * rows, axis=-1, keepdims=True) + EPS_NORM)
    first = rows * scale * gain[...]
    for b in range(dp * tp):
        rest = jnp.concatenate(
            [
                first[:, depth * b + 128 : depth * (b + 1)],
                jnp.zeros((SLOTS, 256 - depth), F32),
            ],
            axis=1,
        )
        msg_ref[b] = jnp.concatenate(
            [first[:, depth * b : depth * b + 128], rest], axis=0
        ).astype(BF16)
    raw_ref[0:SLOTS] = rows.astype(BF16)

    @pl.when(held > SLOTS)
    def _():
        raw[...] = jnp.zeros_like(raw)
        raw[0:SLOTS] = rows

        def take(rank, _):
            picked = lax.broadcasted_iota(jnp.int32, (16, width), 0) == arrive(rank)
            raw[pl.ds(rank, 1), :] = jnp.sum(
                jnp.where(picked, buf[rank].astype(F32), 0.0), axis=0, keepdims=True
            )
            return 0

        lax.fori_loop(SLOTS, held, take, 0)
        raw_ref[...] = raw[...].astype(BF16)


def by_core(rows, dp, per_dp):
    even = lax.axis_index("dp") % 2 == 0
    mine, other = [], []
    for x in range(dp // 2):
        at_even = rows[(2 * x) * per_dp : (2 * x + 1) * per_dp]
        at_odd = rows[(2 * x + 1) * per_dp : (2 * x + 2) * per_dp]
        mine.append(jnp.where(even, at_even, at_odd))
        other.append(jnp.where(even, at_odd, at_even))
    return jnp.concatenate(mine + other, axis=0)


def project_kernel(dp, tp, place_ref, msg_ref, extra_ref, weight_ref, keep_ref, send_ref):
    tokens = place_ref.shape[0]
    per_dp = tokens // dp
    width = HEADS * HEAD
    kv_width = KV_HEADS * HEAD
    slots = dp * tp * SLOTS
    blocks = msg_ref[...].astype(F32)
    place = place_ref[:, 0:1]
    holder, rank = place // tokens, place % tokens
    place = jnp.where(rank < SLOTS, holder * SLOTS + rank, -1)
    select = (lax.broadcasted_iota(jnp.int32, (tokens, slots), 1) == place).astype(BF16)
    extra = extra_ref[...].astype(F32)

    def pick(rows, more):
        rows = rows.reshape(slots, 128).astype(BF16)
        return (jnp.dot(select, rows, preferred_element_type=F32) + more).astype(BF16)

    main = pick(blocks[:, :SLOTS], extra[:, :128])
    rest = pick(blocks[:, SLOTS:], extra[:, 128:])[:, : weight_ref.shape[0] - 128]
    half = tokens // 2

    def dot(at, size):
        return jnp.dot(
            main, weight_ref[0:128, at : at + size], preferred_element_type=F32
        ) + jnp.dot(rest, weight_ref[128:, at : at + size], preferred_element_type=F32)

    my_x, my_tp = lax.axis_index("dp") // 2, lax.axis_index("tp")
    upper = per_dp // 2
    for g in range(tp):
        spans = (
            (0, g * GROUP * HEAD, GROUP * HEAD),
            (GROUP * HEAD, width + g * HEAD, HEAD),
            ((GROUP + 1) * HEAD, width + kv_width + g * HEAD, HEAD),
        )
        away = g ^ my_tp
        in_y, in_z = away % 2, away // 2
        for to, at, size in spans:
            part = dot(at, size)
            cols = slice(to, to + size)
            for x in range(dp // 2):
                in_x = x ^ my_x
                for ref, start in ((keep_ref, per_dp * x), (send_ref, half + per_dp * x)):
                    ref[0, in_x, in_y, in_z, :, cols] = part[start : start + upper]
                    ref[1, in_y, in_x, in_z, :, cols] = part[start + upper : start + per_dp]


def attend_kernel(dp, tp, lengths_ref, qkv_ref, keys_ref, values_ref, msg_ref,
                  keys, values, scores_of, probs_of, weighted_of, joined, key_sems, value_sems):
    rows, span = keys.shape[0], keys.shape[1]
    per_dp = rows * STEPS
    lines = GROUP * per_dp
    my_tp = lax.axis_index("tp")
    depth = HEADS * HEAD // (dp * tp)
    scale = HEAD ** (-0.5)
    nt = (((1,), (1,)), ((), ()))

    def copies(source, target, sems):
        return [
            pltpu.make_async_copy(source.at[r], target.at[r], sems.at[r]) for r in range(rows)
        ]

    key_copies = copies(keys_ref, keys, key_sems)
    value_copies = copies(values_ref, values, value_sems)
    for copy in key_copies + value_copies:
        copy.start()

    line = lax.broadcasted_iota(jnp.int32, (lines, 1), 0) % per_dp
    row_of = line // STEPS
    length = jnp.zeros((lines, 1), jnp.int32)
    for r in range(rows):
        length = jnp.where(row_of == r, lengths_ref[r], length)
    position = my_tp * span + lax.broadcasted_iota(jnp.int32, (lines, span), 1)
    live = position < length
    column = lax.broadcasted_iota(jnp.int32, (lines, per_dp), 1)
    causal = (column // STEPS == row_of) & (column <= line)

    queries = []
    for g in range(KV_HEADS):
        queries.append(
            jnp.concatenate(
                [qkv_ref[g, :, HEAD * h : HEAD * (h + 1)] for h in range(GROUP)], axis=0
            )
        )
    for r in range(rows):
        key_copies[r].wait()
        for g in range(KV_HEADS):
            part = lax.dot_general(
                queries[g],
                keys[r, :, HEAD * g : HEAD * (g + 1)],
                nt,
                preferred_element_type=F32,
            )
            scores_of[g] = part if r == 0 else jnp.where(row_of == r, part, scores_of[g])
    kept = []
    for g in range(KV_HEADS):
        fresh_keys = qkv_ref[g, :, GROUP * HEAD : (GROUP + 1) * HEAD]
        fresh_values = qkv_ref[g, :, (GROUP + 1) * HEAD :]
        scores = jnp.where(live, scores_of[g] * scale, MASK_LOW)
        fresh = lax.dot_general(queries[g], fresh_keys, nt, preferred_element_type=F32) * scale
        seen = causal & (my_tp == g)
        fresh = jnp.where(seen, fresh, MASK_LOW)
        top = jnp.maximum(
            jnp.max(scores, axis=-1, keepdims=True), jnp.max(fresh, axis=-1, keepdims=True)
        )
        probs = jnp.where(live, jnp.exp(scores - top), 0.0)
        fresh_probs = jnp.where(seen, jnp.exp(fresh - top), 0.0)
        total = jnp.sum(probs, axis=-1, keepdims=True)
        total += jnp.sum(fresh_probs, axis=-1, keepdims=True)
        probs_of[g] = probs.astype(BF16)
        weighted_of[g] = jnp.dot(
            fresh_probs.astype(BF16), fresh_values, preferred_element_type=F32
        )
        kept.append((top, total))
    for r in range(rows):
        value_copies[r].wait()
        for g in range(KV_HEADS):
            probs = probs_of[g]
            weighted_of[g] += jnp.dot(
                jnp.where(row_of == r, probs, jnp.zeros_like(probs)),
                values[r, :, HEAD * g : HEAD * (g + 1)],
                preferred_element_type=F32,
            )

    lane = lax.broadcasted_iota(jnp.int32, (per_dp, HEAD), 1)
    levels = jnp.zeros((per_dp, HEAD), F32)
    for g in range(KV_HEADS):
        top, total = kept[g]
        some = total > 0.0
        safe = jnp.where(some, total, 1.0)
        outcome = weighted_of[g] / safe
        logsum = jnp.where(some, top + jnp.log(safe), MASK_LOW)
        for h in range(GROUP):
            head = g * GROUP + h
            joined[:, HEAD * head : HEAD * (head + 1)] = outcome[per_dp * h : per_dp * (h + 1)]
            one = logsum[per_dp * h : per_dp * (h + 1)]
            high = one.astype(BF16).astype(F32)
            middle = (one - high).astype(BF16).astype(F32)
            for i, part in enumerate((high, middle, one - high - middle)):
                levels = jnp.where(lane == 3 * head + i, part, levels)
    for b in range(dp * tp):
        at = depth * b
        turned = pltpu.roll(levels, (depth - 128 - 3 * (at // HEAD)) % 128, 1)
        rest = jnp.concatenate(
            [joined[:, at + 128 : at + depth], jnp.zeros((per_dp, 256 - depth), F32)], axis=1
        )
        rest = jnp.where(lane < depth - 128, rest, turned)
        msg_ref[b] = jnp.concatenate([joined[:, at : at + 128], rest], axis=1).astype(BF16)


def output_kernel(dp, tp, place_ref, msg_ref, weight_ref, raw_ref, keep_ref, send_ref):
    depth = weight_ref.shape[0]
    tokens, per_dp = place_ref.shape[0], msg_ref.shape[1]
    my_block = lax.axis_index("dp") * tp + lax.axis_index("tp")
    edge = HEAD - (depth * my_block) % HEAD
    first_head = lax.broadcasted_iota(jnp.int32, (per_dp, depth), 1) < edge
    merged = []
    for d in range(dp):
        parts, levels = [], []
        for t in range(tp):
            block = msg_ref[d * tp + t].astype(F32)
            stats = [block[:, depth + i : depth + i + 1] for i in range(6)]
            one = stats[0] + stats[1] + stats[2]
            two = stats[3] + stats[4] + stats[5]
            levels.append(jnp.where(first_head, one, two))
            parts.append(block[:, :depth])
        top = functools.reduce(jnp.maximum, levels)
        total = jnp.zeros_like(top)
        weighted = jnp.zeros_like(top)
        for part, lev in zip(parts, levels):
            share = jnp.exp(lev - top)
            total += share
            weighted += share * part
        merged.append(weighted / total)
    attended = by_core(jnp.concatenate(merged, axis=0), dp, per_dp).astype(BF16)
    place = place_ref[:, 0:1] - my_block * tokens
    select = (lax.broadcasted_iota(jnp.int32, (tokens, tokens), 1) == place).astype(BF16)
    half = tokens // 2
    out_width = weight_ref.shape[1] // tp
    for t in range(tp):
        cols = slice(out_width * t, out_width * (t + 1))
        part = jnp.dot(attended, weight_ref[:, cols], preferred_element_type=F32)
        part += jnp.dot(select, raw_ref[:, cols], preferred_element_type=F32)
        for x in range(dp // 2):
            keep_ref[x * tp + t] = part[per_dp * x : per_dp * (x + 1)]
            send_ref[x * tp + t] = part[half + per_dp * x : half + per_dp * (x + 1)]


def finish_kernel(sums_ref, out_ref):
    total = jnp.sum(sums_ref[...].astype(F32), axis=0)
    out_ref[...] = total.reshape(out_ref.shape).astype(BF16)


def whole(shape_count):
    return [pl.BlockSpec(memory_space=pltpu.VMEM)] * shape_count


def on_device_partial(
    dp,
    tp,
    qkv_master,
    qkv_first,
    qkv_second,
    qkv_grad,
    out_master,
    out_first,
    out_second,
    out_grad,
    norm_gain,
    embed_table,
    cache_keys,
    cache_values,
    cache_lengths,
    token_ids,
):
    width = embed_table.shape[1]
    group_rows, span = cache_keys.shape[0], cache_keys.shape[1]
    per_dp = group_rows * STEPS
    tokens = per_dp * dp
    half = dp // 2 * tp
    depth = width // (dp * tp)
    out_width = width // tp
    joined_width = (GROUP + 2) * HEAD

    def granted(size):
        return pltpu.CompilerParams(vmem_limit_bytes=size * MIB)


    core_pairs = [
        (d * tp + t, (d ^ 1) * tp + t) for d in range(dp) for t in range(tp)
    ]
    same_core = [
        [(2 * x + c) * tp + t for x in range(dp // 2) for t in range(tp)] for c in range(2)
    ]

    def other_core(value):
        return lax.ppermute(value, BOTH, core_pairs)

    def neighbour(value, flip):
        pairs = [
            (d * tp + t, (d ^ flip[0]) * tp + (t ^ flip[1])) for d in range(dp) for t in range(tp)
        ]
        return lax.ppermute(value, BOTH, pairs)

    def among_chips(value):
        return lax.all_to_all(value, BOTH, 0, 0, tiled=True, axis_index_groups=same_core)

    message, raw_rows, place, most = pl.pallas_call(
        functools.partial(lookup_kernel, dp, tp),
        out_shape=(
            jax.ShapeDtypeStruct((dp * tp, 2 * SLOTS, 128), BF16),
            jax.ShapeDtypeStruct((tokens, width), BF16),
            jax.ShapeDtypeStruct((tokens, 128), jnp.int32),
            jax.ShapeDtypeStruct((1,), jnp.int32),
        ),
        in_specs=[
            pl.BlockSpec(memory_space=pltpu.SMEM),
            pl.BlockSpec(memory_space=pl.ANY),
            pl.BlockSpec(memory_space=pl.ANY),
        ],
        out_specs=tuple(whole(3)) + (pl.BlockSpec(memory_space=pltpu.SMEM),),
        scratch_shapes=[
            pltpu.VMEM((tokens, 16, width), BF16),
            pltpu.VMEM((1, width), F32),
            pltpu.VMEM((tokens, width), F32),
            pltpu.VMEM((tokens, 128), jnp.int32),
            pltpu.SMEM((tokens + 1,), jnp.int32),
            pltpu.SemaphoreType.DMA((tokens,)),
            pltpu.SemaphoreType.DMA,
        ],
        compiler_params=granted(62),
        name="lookup",
    )(token_ids.T, embed_table, norm_gain.reshape(1, width))

    arrived = lax.all_to_all(message, BOTH, 0, 0, tiled=True)

    def one_more(state):
        k, found = state
        rows = lax.dynamic_slice_in_dim(raw_rows, k * SLOTS, SLOTS, 0).astype(F32)
        meansq = jnp.mean(rows * rows, axis=-1, keepdims=True)
        rows = (rows * lax.rsqrt(meansq + EPS_NORM) * norm_gain).astype(BF16)
        rows = rows.reshape(SLOTS, dp * tp, depth).transpose(1, 0, 2)
        rows = lax.all_to_all(rows, BOTH, 0, 0, tiled=True).reshape(-1, depth)
        holder, rank = place[:, :1] // tokens, place[:, :1] % tokens
        at = jnp.where(rank // SLOTS == k, holder * SLOTS + rank % SLOTS, -1)
        select = (at == jnp.arange(dp * tp * SLOTS, dtype=jnp.int32)).astype(BF16)
        rows = jnp.dot(select, rows, preferred_element_type=F32).astype(BF16)
        return k + 1, found + jnp.pad(rows, ((0, 0), (0, 256 - depth)))

    def all_more(rounds):
        return lax.while_loop(
            lambda state: state[0] <= rounds,
            one_more,
            (jnp.int32(1), jnp.zeros((tokens, 256), BF16)),
        )[1]

    qkv_half = adamw(qkv_master, qkv_first, qkv_second, qkv_grad)[0].astype(BF16)
    out_master_new, out_first_new, out_second_new = adamw(
        out_master, out_first, out_second, out_grad
    )
    out_half = out_master_new.astype(BF16)
    arrived, most = lax.optimization_barrier((arrived, most))
    extra = all_more(most[0] // SLOTS)

    keep, send = pl.pallas_call(
        functools.partial(project_kernel, dp, tp),
        out_shape=(
            jax.ShapeDtypeStruct((2, 2, 2, tp // 2, per_dp // 2, joined_width), F32),
        ) * 2,
        in_specs=whole(4),
        out_specs=tuple(whole(2)),
        compiler_params=granted(16),
        name="project",
    )(place, arrived, extra, qkv_half)
    arrived = other_core(send)

    def fold(across, where):
        pairs = [(mine[0], neighbour(mine[1], flip)) for mine, flip in zip(across, where)]
        return [near + came for near, came in pairs]

    halves = [
        [keep[i, j] + arrived[i, j] for j in range(2)] for i in range(2)
    ]
    halves = fold(halves, ((2, 0), (0, 1)))
    halves = fold(halves, ((0, 1), (2, 0)))
    total = jnp.concatenate(halves, axis=1)
    flip = tp // 2
    while total.shape[0] > 1:
        count = total.shape[0] // 2
        total = total[:count] + neighbour(total[count:], (0, flip))
        flip //= 2
    projected = total[0].astype(BF16)
    joined = lax.all_to_all(
        jnp.broadcast_to(projected[None], (tp,) + projected.shape), "tp", 0, 0, tiled=True
    )

    messages = pl.pallas_call(
        functools.partial(attend_kernel, dp, tp),
        out_shape=jax.ShapeDtypeStruct((dp * tp, per_dp, 256), BF16),
        in_specs=[
            pl.BlockSpec(memory_space=pltpu.SMEM),
            pl.BlockSpec(memory_space=pltpu.VMEM),
            pl.BlockSpec(memory_space=pltpu.HBM),
            pl.BlockSpec(memory_space=pltpu.HBM),
        ],
        out_specs=pl.BlockSpec(memory_space=pltpu.VMEM),
        scratch_shapes=[
            pltpu.VMEM((group_rows, span, cache_keys.shape[2]), BF16),
            pltpu.VMEM((group_rows, span, cache_keys.shape[2]), BF16),
            pltpu.VMEM((KV_HEADS, GROUP * per_dp, span), F32),
            pltpu.VMEM((KV_HEADS, GROUP * per_dp, span), BF16),
            pltpu.VMEM((KV_HEADS, GROUP * per_dp, HEAD), F32),
            pltpu.VMEM((per_dp, width), F32),
            pltpu.SemaphoreType.DMA((group_rows,)),
            pltpu.SemaphoreType.DMA((group_rows,)),
        ],
        compiler_params=granted(56),
        name="attend",
    )(cache_lengths, joined, cache_keys, cache_values)
    arrived = lax.all_to_all(messages, BOTH, 0, 0, tiled=True)

    keep, send = pl.pallas_call(
        functools.partial(output_kernel, dp, tp),
        out_shape=(jax.ShapeDtypeStruct((half, per_dp, out_width), F32),) * 2,
        in_specs=whole(4),
        out_specs=tuple(whole(2)),
        compiler_params=granted(16),
        name="output",
    )(place, arrived, out_half, raw_rows)
    paired, *state = lax.optimization_barrier(
        ((keep + other_core(send)).astype(BF16), qkv_master, qkv_first, qkv_second, qkv_grad)
    )
    sums = among_chips(paired)
    qkv_master_new, qkv_first_new, qkv_second_new = adamw(*state)
    layer_out = pl.pallas_call(
        finish_kernel,
        out_shape=jax.ShapeDtypeStruct((group_rows, STEPS, out_width), BF16),
        in_specs=whole(1),
        out_specs=whole(1)[0],
        compiler_params=granted(16),
        name="finish",
    )(sums)
    return (
        qkv_master_new,
        qkv_first_new,
        qkv_second_new,
        out_master_new,
        out_first_new,
        out_second_new,
        layer_out,
    )


def on_device_general(
    qkv_master,
    qkv_first,
    qkv_second,
    qkv_grad,
    out_master,
    out_first,
    out_second,
    out_grad,
    norm_gain,
    embed_table,
    cache_keys,
    cache_values,
    cache_lengths,
    token_ids,
):
    qkv_master_new, qkv_first_new, qkv_second_new = adamw(
        qkv_master, qkv_first, qkv_second, qkv_grad
    )
    out_master_new, out_first_new, out_second_new = adamw(
        out_master, out_first, out_second, out_grad
    )
    qkv_half = qkv_master_new.astype(jnp.bfloat16)
    out_half = out_master_new.astype(jnp.bfloat16)
    qkv_group, out_group = (
        lax.all_to_all(qkv_half, "tp", split_axis=1, concat_axis=0, tiled=True),
        lax.all_to_all(out_half, "tp", split_axis=1, concat_axis=0, tiled=True),
    )
    qkv_cols, out_cols = (
        lax.all_gather(qkv_group, "dp", axis=0, tiled=True),
        lax.all_gather(out_group, "dp", axis=0, tiled=True),
    )
    width = embed_table.shape[1]
    vocab_rows = embed_table.shape[0]
    group_rows = cache_keys.shape[0]
    first_entry = lax.axis_index(("dp", "tp")) * vocab_rows
    local_ids = token_ids.reshape(-1) - first_entry
    selector = (local_ids[:, None] == jnp.arange(vocab_rows, dtype=jnp.int32)[None, :]).astype(
        jnp.bfloat16
    )
    partial_rows = jnp.dot(selector, embed_table, preferred_element_type=jnp.float32).reshape(
        -1, 2, width
    )
    every_row = lax.psum(partial_rows, ("dp", "tp"))
    own_inputs = lax.dynamic_slice_in_dim(
        every_row, lax.axis_index("dp") * group_rows, group_rows, 0
    )
    meansq = jnp.mean(own_inputs * own_inputs, axis=-1, keepdims=True)
    normed = (own_inputs * lax.rsqrt(meansq + EPS_NORM) * norm_gain).astype(jnp.bfloat16)
    proj_part = jnp.dot(
        normed.reshape(-1, width), qkv_cols, preferred_element_type=jnp.float32
    ).astype(jnp.bfloat16)
    projected = lax.all_gather(proj_part, "tp", axis=1, tiled=True).reshape(group_rows, 2, -1)
    group_size = HEADS // KV_HEADS
    kv_width = KV_HEADS * HEAD
    scale_factor = HEAD ** (-0.5)
    queries = projected[..., :width].reshape(group_rows, 2, KV_HEADS, group_size, HEAD)
    fresh_keys = projected[..., width : width + kv_width].reshape(group_rows, 2, KV_HEADS, HEAD)
    fresh_values = projected[..., width + kv_width :].reshape(group_rows, 2, KV_HEADS, HEAD)
    span = cache_keys.shape[1]
    old_keys = cache_keys.reshape(group_rows, span, KV_HEADS, HEAD)
    old_values = cache_values.reshape(group_rows, span, KV_HEADS, HEAD)
    cache_scores = (
        jnp.einsum("rsghd,rpgd->rsghp", queries, old_keys, preferred_element_type=jnp.float32)
        * scale_factor
    )
    position = lax.axis_index("tp") * span + jnp.arange(span, dtype=jnp.int32)
    live = (position[None, :] < cache_lengths[:, None])[:, None, None, None, :]
    cache_scores = jnp.where(live, cache_scores, MASK_LOW)
    local_top = cache_scores.max(-1)
    cache_probs = jnp.where(live, jnp.exp(cache_scores - local_top[..., None]), 0.0)
    local_total = cache_probs.sum(-1)
    local_weighted = jnp.einsum(
        "rsghp,rpgd->rsghd", cache_probs, old_values, preferred_element_type=jnp.float32
    )
    cache_top = lax.pmax(local_top, "tp")
    rescale = jnp.exp(local_top - cache_top)
    cache_total, cache_weighted = lax.psum(
        (local_total * rescale, local_weighted * rescale[..., None]), "tp"
    )
    fresh_scores = (
        jnp.einsum("rsghd,rjgd->rsghj", queries, fresh_keys, preferred_element_type=jnp.float32)
        * scale_factor
    )
    causal = jnp.arange(2, dtype=jnp.int32)[None, :] <= jnp.arange(2, dtype=jnp.int32)[:, None]
    causal = causal[None, :, None, None, :]
    fresh_scores = jnp.where(causal, fresh_scores, MASK_LOW)
    highest = jnp.maximum(cache_top, fresh_scores.max(-1))
    cache_scale = jnp.exp(cache_top - highest)
    fresh_probs = jnp.where(causal, jnp.exp(fresh_scores - highest[..., None]), 0.0)
    totals = cache_total * cache_scale + fresh_probs.sum(-1)
    weighted = cache_weighted * cache_scale[..., None]
    weighted = weighted + jnp.einsum(
        "rsghj,rjgd->rsghd", fresh_probs, fresh_values.astype(jnp.float32)
    )
    attended = (weighted / totals[..., None]).reshape(group_rows * 2, width).astype(jnp.bfloat16)
    out_width = out_cols.shape[1]
    mixed = jnp.dot(attended, out_cols, preferred_element_type=jnp.float32).reshape(
        group_rows, 2, out_width
    )
    residual_cols = lax.dynamic_slice_in_dim(
        own_inputs, lax.axis_index("tp") * out_width, out_width, 2
    )
    layer_out = (residual_cols + mixed).astype(jnp.bfloat16)
    return (
        qkv_master_new,
        qkv_first_new,
        qkv_second_new,
        out_master_new,
        out_first_new,
        out_second_new,
        layer_out,
    )


def solution(mesh):
    dp, tp = mesh.shape["dp"], mesh.shape["tp"]
    placed = (
        P(("dp", "tp"), None),
        P(("dp", "tp"), None),
        P(("dp", "tp"), None),
        P(("dp", "tp"), None),
        P(("dp", "tp"), None),
        P(("dp", "tp"), None),
        P(("dp", "tp"), None),
        P(("dp", "tp"), None),
        P(),
        P(("dp", "tp"), None),
        P("dp", "tp", None),
        P("dp", "tp", None),
        P("dp"),
        P(),
    )
    body = on_device_general
    if (dp, tp) == (4, KV_HEADS):
        body = functools.partial(on_device_partial, dp, tp)
    return jax.shard_map(
        body,
        mesh=mesh,
        in_specs=placed,
        out_specs=(
            P(("dp", "tp"), None),
            P(("dp", "tp"), None),
            P(("dp", "tp"), None),
            P(("dp", "tp"), None),
            P(("dp", "tp"), None),
            P(("dp", "tp"), None),
            P("dp", None, "tp"),
        ),
        check_vma=False,
    )
```

```python
import functools

import jax
import jax.numpy as jnp
from jax import lax
from jax.experimental import pallas as pl
from jax.experimental.pallas import tpu as pltpu
from jax.sharding import PartitionSpec as P

HEADS = 40
KV_HEADS = 8
HEAD = 128
GROUP = HEADS // KV_HEADS
STEPS = 2
SLOTS = 8


BETA_ONE = 0.9
BETA_TWO = 0.95
LEARN_RATE = 0.004
WEIGHT_DECAY = 0.1
EPS_ADAM = 1e-08
EPS_NORM = 1e-06
CORR_ONE = 1.0 - 0.9**10
CORR_TWO = 1.0 - 0.95**10
MASK_LOW = -1e30
BOTH = ("dp", "tp")
F32 = jnp.float32
BF16 = jnp.bfloat16
MIB = 1024 * 1024


def adamw(master, first, second, grad):
    gradient = grad.astype(jnp.float32)
    first_new = BETA_ONE * first + (1.0 - BETA_ONE) * gradient
    second_new = BETA_TWO * second + (1.0 - BETA_TWO) * gradient * gradient
    update = first_new / CORR_ONE / (jnp.sqrt(second_new / CORR_TWO) + EPS_ADAM)
    master_new = master - LEARN_RATE * (update + WEIGHT_DECAY * master)
    return (master_new, first_new, second_new)


def lookup_kernel(dp, tp, ids_ref, table_ref, gain_ref, msg_ref, raw_ref, place_ref, most_ref,
                  buf, gain, raw, column, entries, sems, gain_sem):
    tokens, width = raw.shape
    per_dp = tokens // dp
    vocab_rows = table_ref.shape[0]
    whole = vocab_rows // 16 * 16
    left = vocab_rows - whole
    depth = width // (dp * tp)
    my_core = lax.axis_index("dp") % 2
    base = (lax.axis_index("dp") * tp + lax.axis_index("tp")) * vocab_rows
    gain_copy = pltpu.make_async_copy(gain_ref, gain, gain_sem)
    gain_copy.start()

    def whole_rows(entry, rank):
        start = pl.multiple_of(entry // 16 * 16, 16)
        return pltpu.make_async_copy(
            table_ref.at[pl.ds(start, 16)], buf.at[rank], sems.at[rank]
        )

    def last_rows(rank):
        return pltpu.make_async_copy(
            table_ref.at[pl.ds(whole, left)], buf.at[rank, pl.ds(0, left)], sems.at[rank]
        )

    def look(t, held):
        identity = ids_ref[t % STEPS, t // STEPS]
        group = t // per_dp
        line = (group % 2 ^ my_core) * (tokens // 2) + group // 2 * per_dp + t % per_dp
        column[pl.ds(line, 1), :] = jnp.full((1, 128), identity, jnp.int32)
        entry = identity - base
        entries[held] = entry
        mine = jnp.logical_and(entry >= 0, entry < vocab_rows)
        return held + mine.astype(jnp.int32)

    held = jnp.int32(0)
    for t in range(tokens):
        held = look(t, held)

    def fetch(rank, _):
        entry = entries[rank]

        @pl.when(entry < whole)
        def _():
            whole_rows(entry, rank).start()

        if left:
            @pl.when(entry >= whole)
            def _():
                last_rows(rank).start()

        return 0

    buf[0:SLOTS] = jnp.zeros((SLOTS, 16, width), BF16)
    lax.fori_loop(0, held, fetch, 0)
    raw_ref[SLOTS:] = jnp.zeros((tokens - SLOTS, width), BF16)
    line = lax.broadcasted_iota(jnp.int32, (tokens, 128), 0)
    inside = line % (tokens // 2)
    order = (inside // per_dp * 2 + (line // (tokens // 2) ^ my_core)) * per_dp + line % per_dp
    identity = column[...].astype(F32)
    holder = jnp.floor(identity * (1.0 / vocab_rows))
    holder = jnp.where(holder * vocab_rows > identity, holder - 1.0, holder)
    holder = jnp.where((holder + 1.0) * vocab_rows <= identity, holder + 1.0, holder)
    key = holder * tokens + order.astype(F32)
    turned = jnp.transpose(
        jnp.concatenate([key, jnp.full((128 - tokens, 128), -1.0, F32)], axis=0)
    )[0:1, :]
    before = (turned >= holder * tokens) & (turned < key)
    rank = jnp.sum(before.astype(F32), axis=1, keepdims=True)
    place_ref[...] = (holder * tokens + rank).astype(jnp.int32)
    most_ref[0] = jnp.max(rank).astype(jnp.int32)

    def arrive(rank):
        entry = entries[rank]

        @pl.when(entry < whole)
        def _():
            whole_rows(entry, rank).wait()

        if left:
            @pl.when(entry >= whole)
            def _():
                last_rows(rank).wait()

        return entry % 16

    source = jnp.full((SLOTS, 1), -1, jnp.int32)
    slot = lax.broadcasted_iota(jnp.int32, (SLOTS, 1), 0)
    for rank in range(SLOTS):
        @pl.when(rank < held)
        def _():
            arrive(rank)

        at = jnp.where(rank < held, rank * 16 + entries[rank] % 16, -1)
        source = jnp.where(slot == rank, at, source)
    select = (
        lax.broadcasted_iota(jnp.int32, (SLOTS, SLOTS * 16), 1) == source
    ).astype(BF16)
    rows = jnp.dot(
        select, buf[0:SLOTS].reshape(SLOTS * 16, width), preferred_element_type=F32
    )
    gain_copy.wait()
    scale = lax.rsqrt(jnp.mean(rows * rows, axis=-1, keepdims=True) + EPS_NORM)
    first = rows * scale * gain[...]
    for b in range(dp * tp):
        rest = jnp.concatenate(
            [
                first[:, depth * b + 128 : depth * (b + 1)],
                jnp.zeros((SLOTS, 256 - depth), F32),
            ],
            axis=1,
        )
        msg_ref[b] = jnp.concatenate(
            [first[:, depth * b : depth * b + 128], rest], axis=0
        ).astype(BF16)
    raw_ref[0:SLOTS] = rows.astype(BF16)

    @pl.when(held > SLOTS)
    def _():
        raw[...] = jnp.zeros_like(raw)
        raw[0:SLOTS] = rows

        def take(rank, _):
            picked = lax.broadcasted_iota(jnp.int32, (16, width), 0) == arrive(rank)
            raw[pl.ds(rank, 1), :] = jnp.sum(
                jnp.where(picked, buf[rank].astype(F32), 0.0), axis=0, keepdims=True
            )
            return 0

        lax.fori_loop(SLOTS, held, take, 0)
        raw_ref[...] = raw[...].astype(BF16)


def by_core(rows, dp, per_dp):
    even = lax.axis_index("dp") % 2 == 0
    mine, other = [], []
    for x in range(dp // 2):
        at_even = rows[(2 * x) * per_dp : (2 * x + 1) * per_dp]
        at_odd = rows[(2 * x + 1) * per_dp : (2 * x + 2) * per_dp]
        mine.append(jnp.where(even, at_even, at_odd))
        other.append(jnp.where(even, at_odd, at_even))
    return jnp.concatenate(mine + other, axis=0)


def project_kernel(dp, tp, place_ref, msg_ref, extra_ref, weight_ref, keep_ref, send_ref):
    tokens = place_ref.shape[0]
    per_dp = tokens // dp
    width = HEADS * HEAD
    kv_width = KV_HEADS * HEAD
    slots = dp * tp * SLOTS
    blocks = msg_ref[...].astype(F32)
    place = place_ref[:, 0:1]
    holder, rank = place // tokens, place % tokens
    place = jnp.where(rank < SLOTS, holder * SLOTS + rank, -1)
    select = (lax.broadcasted_iota(jnp.int32, (tokens, slots), 1) == place).astype(BF16)
    extra = extra_ref[...].astype(F32)

    def pick(rows, more):
        rows = rows.reshape(slots, 128).astype(BF16)
        return (jnp.dot(select, rows, preferred_element_type=F32) + more).astype(BF16)

    main = pick(blocks[:, :SLOTS], extra[:, :128])
    rest = pick(blocks[:, SLOTS:], extra[:, 128:])[:, : weight_ref.shape[0] - 128]
    half = tokens // 2

    def dot(at, size):
        return jnp.dot(
            main, weight_ref[0:128, at : at + size], preferred_element_type=F32
        ) + jnp.dot(rest, weight_ref[128:, at : at + size], preferred_element_type=F32)

    my_x, my_tp = lax.axis_index("dp") // 2, lax.axis_index("tp")
    upper = per_dp // 2
    for g in range(tp):
        spans = (
            (0, g * GROUP * HEAD, GROUP * HEAD),
            (GROUP * HEAD, width + g * HEAD, HEAD),
            ((GROUP + 1) * HEAD, width + kv_width + g * HEAD, HEAD),
        )
        away = g ^ my_tp
        in_y, in_z = away % 2, away // 4 + away // 2 % 2 * 2
        for to, at, size in spans:
            part = dot(at, size)
            cols = slice(to, to + size)
            for x in range(dp // 2):
                in_x = x ^ my_x
                for ref, start in ((keep_ref, per_dp * x), (send_ref, half + per_dp * x)):
                    ref[0, in_x, in_y, in_z, :, cols] = part[start : start + upper]
                    ref[1, in_y, in_x, in_z, :, cols] = part[start + upper : start + per_dp]


def attend_kernel(dp, tp, lengths_ref, qkv_ref, keys_ref, values_ref, msg_ref,
                  keys, values, scores_of, probs_of, weighted_of, joined, key_sems, value_sems):
    rows, span = keys.shape[0], keys.shape[1]
    per_dp = rows * STEPS
    lines = GROUP * per_dp
    my_tp = lax.axis_index("tp")
    depth = HEADS * HEAD // (dp * tp)
    scale = HEAD ** (-0.5)
    nt = (((1,), (1,)), ((), ()))

    def copies(source, target, sems):
        return [
            pltpu.make_async_copy(source.at[r], target.at[r], sems.at[r]) for r in range(rows)
        ]

    key_copies = copies(keys_ref, keys, key_sems)
    value_copies = copies(values_ref, values, value_sems)
    for copy in key_copies + value_copies:
        copy.start()

    line = lax.broadcasted_iota(jnp.int32, (lines, 1), 0) % per_dp
    row_of = line // STEPS
    length = jnp.zeros((lines, 1), jnp.int32)
    for r in range(rows):
        length = jnp.where(row_of == r, lengths_ref[r], length)
    position = my_tp * span + lax.broadcasted_iota(jnp.int32, (lines, span), 1)
    live = position < length
    column = lax.broadcasted_iota(jnp.int32, (lines, per_dp), 1)
    causal = (column // STEPS == row_of) & (column <= line)

    queries = []
    for g in range(KV_HEADS):
        queries.append(
            jnp.concatenate(
                [qkv_ref[g, :, HEAD * h : HEAD * (h + 1)] for h in range(GROUP)], axis=0
            )
        )
    for r in range(rows):
        key_copies[r].wait()
        for g in range(KV_HEADS):
            part = lax.dot_general(
                queries[g],
                keys[r, :, HEAD * g : HEAD * (g + 1)],
                nt,
                preferred_element_type=F32,
            )
            scores_of[g] = part if r == 0 else jnp.where(row_of == r, part, scores_of[g])
    kept = []
    for g in range(KV_HEADS):
        fresh_keys = qkv_ref[g, :, GROUP * HEAD : (GROUP + 1) * HEAD]
        fresh_values = qkv_ref[g, :, (GROUP + 1) * HEAD :]
        scores = jnp.where(live, scores_of[g] * scale, MASK_LOW)
        fresh = lax.dot_general(queries[g], fresh_keys, nt, preferred_element_type=F32) * scale
        seen = causal & (my_tp == g)
        fresh = jnp.where(seen, fresh, MASK_LOW)
        top = jnp.maximum(
            jnp.max(scores, axis=-1, keepdims=True), jnp.max(fresh, axis=-1, keepdims=True)
        )
        probs = jnp.where(live, jnp.exp(scores - top), 0.0)
        fresh_probs = jnp.where(seen, jnp.exp(fresh - top), 0.0)
        total = jnp.sum(probs, axis=-1, keepdims=True)
        total += jnp.sum(fresh_probs, axis=-1, keepdims=True)
        probs_of[g] = probs.astype(BF16)
        weighted_of[g] = jnp.dot(
            fresh_probs.astype(BF16), fresh_values, preferred_element_type=F32
        )
        kept.append((top, total))
    for r in range(rows):
        value_copies[r].wait()
        for g in range(KV_HEADS):
            probs = probs_of[g]
            weighted_of[g] += jnp.dot(
                jnp.where(row_of == r, probs, jnp.zeros_like(probs)),
                values[r, :, HEAD * g : HEAD * (g + 1)],
                preferred_element_type=F32,
            )

    lane = lax.broadcasted_iota(jnp.int32, (per_dp, HEAD), 1)
    levels = jnp.zeros((per_dp, HEAD), F32)
    for g in range(KV_HEADS):
        top, total = kept[g]
        some = total > 0.0
        safe = jnp.where(some, total, 1.0)
        outcome = weighted_of[g] / safe
        logsum = jnp.where(some, top + jnp.log(safe), MASK_LOW)
        for h in range(GROUP):
            head = g * GROUP + h
            joined[:, HEAD * head : HEAD * (head + 1)] = outcome[per_dp * h : per_dp * (h + 1)]
            one = logsum[per_dp * h : per_dp * (h + 1)]
            high = one.astype(BF16).astype(F32)
            middle = (one - high).astype(BF16).astype(F32)
            for i, part in enumerate((high, middle, one - high - middle)):
                levels = jnp.where(lane == 3 * head + i, part, levels)
    for b in range(dp * tp):
        at = depth * b
        turned = pltpu.roll(levels, (depth - 128 - 3 * (at // HEAD)) % 128, 1)
        rest = jnp.concatenate(
            [joined[:, at + 128 : at + depth], jnp.zeros((per_dp, 256 - depth), F32)], axis=1
        )
        rest = jnp.where(lane < depth - 128, rest, turned)
        msg_ref[b] = jnp.concatenate([joined[:, at : at + 128], rest], axis=1).astype(BF16)


def output_kernel(dp, tp, place_ref, msg_ref, weight_ref, raw_ref, keep_ref, send_ref):
    depth = weight_ref.shape[0]
    tokens, per_dp = place_ref.shape[0], msg_ref.shape[1]
    my_block = lax.axis_index("dp") * tp + lax.axis_index("tp")
    edge = HEAD - (depth * my_block) % HEAD
    first_head = lax.broadcasted_iota(jnp.int32, (per_dp, depth), 1) < edge
    merged = []
    for d in range(dp):
        parts, levels = [], []
        for t in range(tp):
            block = msg_ref[d * tp + t].astype(F32)
            stats = [block[:, depth + i : depth + i + 1] for i in range(6)]
            one = stats[0] + stats[1] + stats[2]
            two = stats[3] + stats[4] + stats[5]
            levels.append(jnp.where(first_head, one, two))
            parts.append(block[:, :depth])
        top = functools.reduce(jnp.maximum, levels)
        total = jnp.zeros_like(top)
        weighted = jnp.zeros_like(top)
        for part, lev in zip(parts, levels):
            share = jnp.exp(lev - top)
            total += share
            weighted += share * part
        merged.append(weighted / total)
    attended = by_core(jnp.concatenate(merged, axis=0), dp, per_dp).astype(BF16)
    place = place_ref[:, 0:1] - my_block * tokens
    select = (lax.broadcasted_iota(jnp.int32, (tokens, tokens), 1) == place).astype(BF16)
    half = tokens // 2
    out_width = weight_ref.shape[1] // tp
    for t in range(tp):
        cols = slice(out_width * t, out_width * (t + 1))
        part = jnp.dot(attended, weight_ref[:, cols], preferred_element_type=F32)
        part += jnp.dot(select, raw_ref[:, cols], preferred_element_type=F32)
        for x in range(dp // 2):
            keep_ref[x * tp + t] = part[per_dp * x : per_dp * (x + 1)]
            send_ref[x * tp + t] = part[half + per_dp * x : half + per_dp * (x + 1)]


def finish_kernel(sums_ref, out_ref):
    total = jnp.sum(sums_ref[...].astype(F32), axis=0)
    out_ref[...] = total.reshape(out_ref.shape).astype(BF16)


def whole(shape_count):
    return [pl.BlockSpec(memory_space=pltpu.VMEM)] * shape_count


def on_device_partial(
    dp,
    tp,
    qkv_master,
    qkv_first,
    qkv_second,
    qkv_grad,
    out_master,
    out_first,
    out_second,
    out_grad,
    norm_gain,
    embed_table,
    cache_keys,
    cache_values,
    cache_lengths,
    token_ids,
):
    width = embed_table.shape[1]
    group_rows, span = cache_keys.shape[0], cache_keys.shape[1]
    per_dp = group_rows * STEPS
    tokens = per_dp * dp
    half = dp // 2 * tp
    depth = width // (dp * tp)
    out_width = width // tp
    joined_width = (GROUP + 2) * HEAD

    def granted(size):
        return pltpu.CompilerParams(vmem_limit_bytes=size * MIB)


    core_pairs = [
        (d * tp + t, (d ^ 1) * tp + t) for d in range(dp) for t in range(tp)
    ]
    same_core = [
        [(2 * x + c) * tp + t for x in range(dp // 2) for t in range(tp)] for c in range(2)
    ]

    def other_core(value):
        return lax.ppermute(value, BOTH, core_pairs)

    def neighbour(value, flip):
        pairs = [
            (d * tp + t, (d ^ flip[0]) * tp + (t ^ flip[1])) for d in range(dp) for t in range(tp)
        ]
        return lax.ppermute(value, BOTH, pairs)

    def among_chips(value):
        return lax.all_to_all(value, BOTH, 0, 0, tiled=True, axis_index_groups=same_core)

    message, raw_rows, place, most = pl.pallas_call(
        functools.partial(lookup_kernel, dp, tp),
        out_shape=(
            jax.ShapeDtypeStruct((dp * tp, 2 * SLOTS, 128), BF16),
            jax.ShapeDtypeStruct((tokens, width), BF16),
            jax.ShapeDtypeStruct((tokens, 128), jnp.int32),
            jax.ShapeDtypeStruct((1,), jnp.int32),
        ),
        in_specs=[
            pl.BlockSpec(memory_space=pltpu.SMEM),
            pl.BlockSpec(memory_space=pl.ANY),
            pl.BlockSpec(memory_space=pl.ANY),
        ],
        out_specs=tuple(whole(3)) + (pl.BlockSpec(memory_space=pltpu.SMEM),),
        scratch_shapes=[
            pltpu.VMEM((tokens, 16, width), BF16),
            pltpu.VMEM((1, width), F32),
            pltpu.VMEM((tokens, width), F32),
            pltpu.VMEM((tokens, 128), jnp.int32),
            pltpu.SMEM((tokens + 1,), jnp.int32),
            pltpu.SemaphoreType.DMA((tokens,)),
            pltpu.SemaphoreType.DMA,
        ],
        compiler_params=granted(62),
        name="lookup",
    )(token_ids.T, embed_table, norm_gain.reshape(1, width))

    arrived = lax.all_to_all(message, BOTH, 0, 0, tiled=True)

    def one_more(state):
        k, found = state
        rows = lax.dynamic_slice_in_dim(raw_rows, k * SLOTS, SLOTS, 0).astype(F32)
        meansq = jnp.mean(rows * rows, axis=-1, keepdims=True)
        rows = (rows * lax.rsqrt(meansq + EPS_NORM) * norm_gain).astype(BF16)
        rows = rows.reshape(SLOTS, dp * tp, depth).transpose(1, 0, 2)
        rows = lax.all_to_all(rows, BOTH, 0, 0, tiled=True).reshape(-1, depth)
        holder, rank = place[:, :1] // tokens, place[:, :1] % tokens
        at = jnp.where(rank // SLOTS == k, holder * SLOTS + rank % SLOTS, -1)
        select = (at == jnp.arange(dp * tp * SLOTS, dtype=jnp.int32)).astype(BF16)
        rows = jnp.dot(select, rows, preferred_element_type=F32).astype(BF16)
        return k + 1, found + jnp.pad(rows, ((0, 0), (0, 256 - depth)))

    def all_more(rounds):
        return lax.while_loop(
            lambda state: state[0] <= rounds,
            one_more,
            (jnp.int32(1), jnp.zeros((tokens, 256), BF16)),
        )[1]

    qkv_half = adamw(qkv_master, qkv_first, qkv_second, qkv_grad)[0].astype(BF16)
    out_master_new, out_first_new, out_second_new = adamw(
        out_master, out_first, out_second, out_grad
    )
    out_half = out_master_new.astype(BF16)
    arrived, most = lax.optimization_barrier((arrived, most))
    extra = all_more(most[0] // SLOTS)

    keep, send = pl.pallas_call(
        functools.partial(project_kernel, dp, tp),
        out_shape=(
            jax.ShapeDtypeStruct((2, 2, 2, tp // 2, per_dp // 2, joined_width), F32),
        ) * 2,
        in_specs=whole(4),
        out_specs=tuple(whole(2)),
        compiler_params=granted(16),
        name="project",
    )(place, arrived, extra, qkv_half)
    arrived = other_core(send)

    def fold(across, where):
        pairs = [(mine[0], neighbour(mine[1], flip)) for mine, flip in zip(across, where)]
        return [near + came for near, came in pairs]

    halves = [
        [keep[i, j] + arrived[i, j] for j in range(2)] for i in range(2)
    ]
    halves = fold(halves, ((2, 0), (0, 1)))
    halves = fold(halves, ((0, 1), (2, 0)))
    total = jnp.concatenate(halves, axis=1)
    flip = 2
    while total.shape[0] > 1:
        count = total.shape[0] // 2
        total = total[:count] + neighbour(total[count:], (0, flip))
        flip *= 2
    projected = total[0].astype(BF16)
    joined = lax.all_to_all(
        jnp.broadcast_to(projected[None], (tp,) + projected.shape), "tp", 0, 0, tiled=True
    )

    messages = pl.pallas_call(
        functools.partial(attend_kernel, dp, tp),
        out_shape=jax.ShapeDtypeStruct((dp * tp, per_dp, 256), BF16),
        in_specs=[
            pl.BlockSpec(memory_space=pltpu.SMEM),
            pl.BlockSpec(memory_space=pltpu.VMEM),
            pl.BlockSpec(memory_space=pltpu.HBM),
            pl.BlockSpec(memory_space=pltpu.HBM),
        ],
        out_specs=pl.BlockSpec(memory_space=pltpu.VMEM),
        scratch_shapes=[
            pltpu.VMEM((group_rows, span, cache_keys.shape[2]), BF16),
            pltpu.VMEM((group_rows, span, cache_keys.shape[2]), BF16),
            pltpu.VMEM((KV_HEADS, GROUP * per_dp, span), F32),
            pltpu.VMEM((KV_HEADS, GROUP * per_dp, span), BF16),
            pltpu.VMEM((KV_HEADS, GROUP * per_dp, HEAD), F32),
            pltpu.VMEM((per_dp, width), F32),
            pltpu.SemaphoreType.DMA((group_rows,)),
            pltpu.SemaphoreType.DMA((group_rows,)),
        ],
        compiler_params=granted(56),
        name="attend",
    )(cache_lengths, joined, cache_keys, cache_values)
    arrived = lax.all_to_all(messages, BOTH, 0, 0, tiled=True)

    keep, send = pl.pallas_call(
        functools.partial(output_kernel, dp, tp),
        out_shape=(jax.ShapeDtypeStruct((half, per_dp, out_width), F32),) * 2,
        in_specs=whole(4),
        out_specs=tuple(whole(2)),
        compiler_params=granted(16),
        name="output",
    )(place, arrived, out_half, raw_rows)
    paired, *state = lax.optimization_barrier(
        ((keep + other_core(send)).astype(BF16), qkv_master, qkv_first, qkv_second, qkv_grad)
    )
    sums = among_chips(paired)
    qkv_master_new, qkv_first_new, qkv_second_new = adamw(*state)
    layer_out = pl.pallas_call(
        finish_kernel,
        out_shape=jax.ShapeDtypeStruct((group_rows, STEPS, out_width), BF16),
        in_specs=whole(1),
        out_specs=whole(1)[0],
        compiler_params=granted(16),
        name="finish",
    )(sums)
    return (
        qkv_master_new,
        qkv_first_new,
        qkv_second_new,
        out_master_new,
        out_first_new,
        out_second_new,
        layer_out,
    )


def on_device_general(
    qkv_master,
    qkv_first,
    qkv_second,
    qkv_grad,
    out_master,
    out_first,
    out_second,
    out_grad,
    norm_gain,
    embed_table,
    cache_keys,
    cache_values,
    cache_lengths,
    token_ids,
):
    qkv_master_new, qkv_first_new, qkv_second_new = adamw(
        qkv_master, qkv_first, qkv_second, qkv_grad
    )
    out_master_new, out_first_new, out_second_new = adamw(
        out_master, out_first, out_second, out_grad
    )
    qkv_half = qkv_master_new.astype(jnp.bfloat16)
    out_half = out_master_new.astype(jnp.bfloat16)
    qkv_group, out_group = (
        lax.all_to_all(qkv_half, "tp", split_axis=1, concat_axis=0, tiled=True),
        lax.all_to_all(out_half, "tp", split_axis=1, concat_axis=0, tiled=True),
    )
    qkv_cols, out_cols = (
        lax.all_gather(qkv_group, "dp", axis=0, tiled=True),
        lax.all_gather(out_group, "dp", axis=0, tiled=True),
    )
    width = embed_table.shape[1]
    vocab_rows = embed_table.shape[0]
    group_rows = cache_keys.shape[0]
    first_entry = lax.axis_index(("dp", "tp")) * vocab_rows
    local_ids = token_ids.reshape(-1) - first_entry
    selector = (local_ids[:, None] == jnp.arange(vocab_rows, dtype=jnp.int32)[None, :]).astype(
        jnp.bfloat16
    )
    partial_rows = jnp.dot(selector, embed_table, preferred_element_type=jnp.float32).reshape(
        -1, 2, width
    )
    every_row = lax.psum(partial_rows, ("dp", "tp"))
    own_inputs = lax.dynamic_slice_in_dim(
        every_row, lax.axis_index("dp") * group_rows, group_rows, 0
    )
    meansq = jnp.mean(own_inputs * own_inputs, axis=-1, keepdims=True)
    normed = (own_inputs * lax.rsqrt(meansq + EPS_NORM) * norm_gain).astype(jnp.bfloat16)
    proj_part = jnp.dot(
        normed.reshape(-1, width), qkv_cols, preferred_element_type=jnp.float32
    ).astype(jnp.bfloat16)
    projected = lax.all_gather(proj_part, "tp", axis=1, tiled=True).reshape(group_rows, 2, -1)
    group_size = HEADS // KV_HEADS
    kv_width = KV_HEADS * HEAD
    scale_factor = HEAD ** (-0.5)
    queries = projected[..., :width].reshape(group_rows, 2, KV_HEADS, group_size, HEAD)
    fresh_keys = projected[..., width : width + kv_width].reshape(group_rows, 2, KV_HEADS, HEAD)
    fresh_values = projected[..., width + kv_width :].reshape(group_rows, 2, KV_HEADS, HEAD)
    span = cache_keys.shape[1]
    old_keys = cache_keys.reshape(group_rows, span, KV_HEADS, HEAD)
    old_values = cache_values.reshape(group_rows, span, KV_HEADS, HEAD)
    cache_scores = (
        jnp.einsum("rsghd,rpgd->rsghp", queries, old_keys, preferred_element_type=jnp.float32)
        * scale_factor
    )
    position = lax.axis_index("tp") * span + jnp.arange(span, dtype=jnp.int32)
    live = (position[None, :] < cache_lengths[:, None])[:, None, None, None, :]
    cache_scores = jnp.where(live, cache_scores, MASK_LOW)
    local_top = cache_scores.max(-1)
    cache_probs = jnp.where(live, jnp.exp(cache_scores - local_top[..., None]), 0.0)
    local_total = cache_probs.sum(-1)
    local_weighted = jnp.einsum(
        "rsghp,rpgd->rsghd", cache_probs, old_values, preferred_element_type=jnp.float32
    )
    cache_top = lax.pmax(local_top, "tp")
    rescale = jnp.exp(local_top - cache_top)
    cache_total, cache_weighted = lax.psum(
        (local_total * rescale, local_weighted * rescale[..., None]), "tp"
    )
    fresh_scores = (
        jnp.einsum("rsghd,rjgd->rsghj", queries, fresh_keys, preferred_element_type=jnp.float32)
        * scale_factor
    )
    causal = jnp.arange(2, dtype=jnp.int32)[None, :] <= jnp.arange(2, dtype=jnp.int32)[:, None]
    causal = causal[None, :, None, None, :]
    fresh_scores = jnp.where(causal, fresh_scores, MASK_LOW)
    highest = jnp.maximum(cache_top, fresh_scores.max(-1))
    cache_scale = jnp.exp(cache_top - highest)
    fresh_probs = jnp.where(causal, jnp.exp(fresh_scores - highest[..., None]), 0.0)
    totals = cache_total * cache_scale + fresh_probs.sum(-1)
    weighted = cache_weighted * cache_scale[..., None]
    weighted = weighted + jnp.einsum(
        "rsghj,rjgd->rsghd", fresh_probs, fresh_values.astype(jnp.float32)
    )
    attended = (weighted / totals[..., None]).reshape(group_rows * 2, width).astype(jnp.bfloat16)
    out_width = out_cols.shape[1]
    mixed = jnp.dot(attended, out_cols, preferred_element_type=jnp.float32).reshape(
        group_rows, 2, out_width
    )
    residual_cols = lax.dynamic_slice_in_dim(
        own_inputs, lax.axis_index("tp") * out_width, out_width, 2
    )
    layer_out = (residual_cols + mixed).astype(jnp.bfloat16)
    return (
        qkv_master_new,
        qkv_first_new,
        qkv_second_new,
        out_master_new,
        out_first_new,
        out_second_new,
        layer_out,
    )


def solution(mesh):
    dp, tp = mesh.shape["dp"], mesh.shape["tp"]
    placed = (
        P(("dp", "tp"), None),
        P(("dp", "tp"), None),
        P(("dp", "tp"), None),
        P(("dp", "tp"), None),
        P(("dp", "tp"), None),
        P(("dp", "tp"), None),
        P(("dp", "tp"), None),
        P(("dp", "tp"), None),
        P(),
        P(("dp", "tp"), None),
        P("dp", "tp", None),
        P("dp", "tp", None),
        P("dp"),
        P(),
    )
    body = on_device_general
    if (dp, tp) == (4, KV_HEADS):
        body = functools.partial(on_device_partial, dp, tp)
    return jax.shard_map(
        body,
        mesh=mesh,
        in_specs=placed,
        out_specs=(
            P(("dp", "tp"), None),
            P(("dp", "tp"), None),
            P(("dp", "tp"), None),
            P(("dp", "tp"), None),
            P(("dp", "tp"), None),
            P(("dp", "tp"), None),
            P("dp", None, "tp"),
        ),
        check_vma=False,
    )
```
